128 devices in a mesh: seq: 16 (over z, y), exp: 8 (over x, core).
Axes of the slice: x: 4, y: 4, z: 4, core: 2. Of those that a mesh axis runs over, the one named last changes fastest.
Arguments:
- hidden_in: bfloat16 [2048, 6144], P(('seq', 'exp')), may hold values from -6 to 6
- queries: bfloat16 [2048, 8192], P('seq', 'exp'), may hold values from -4 to 4
- key_rows: bfloat16 [2048, 8192], P('seq', 'exp'), may hold values from -4 to 4
- value_rows: bfloat16 [2048, 8192], P('seq', 'exp'), may hold values from -6 to 6
- out_gate: bfloat16 [2048, 8192], P('seq', 'exp'), may hold values from -6 to 6
- log_decay: float32 [64, 2048], P('exp', 'seq'), may hold values from -1 to 0
- attn_gain: float32 [8192], P('exp'), may hold values from 0.25 to 1.75
- out_weight: bfloat16 [8192, 6144], P('exp'), may hold values from -0.0625 to 0.0625
- ffn_gain: float32 [6144], replicated, may hold values from 0.25 to 1.75
- routes: int32 [2048, 2], P(('seq', 'exp')), may hold values from 0 to 7, all different within a row; in each aligned block of 16 rows (0 to 15, 16 to 31, ...) at most 8 rows name the same one
- combine_weight: float32 [2048, 2], P(('seq', 'exp')), may hold values from 0.2 to 1
- gate_weight: bfloat16 [8, 6144, 4608], P('exp', None, 'seq'), may hold values from -0.078125 to 0.078125
- up_weight: bfloat16 [8, 6144, 4608], P('exp', None, 'seq'), may hold values from -0.078125 to 0.078125
- down_weight: bfloat16 [8, 4608, 6144], P('exp', 'seq'), may hold values from -0.09375 to 0.09375
Outputs:
- layer_out: bfloat16 [2048, 6144], P(('seq', 'exp'))
The draws below stay inside these ranges and needn't reach their ends.
Inputs may be any that keep to these rules, and one draw needn't show every extreme that they name: `routes`: the two experts of a token differ; in each aligned block of 16 tokens no expert is named more than 8 times, and this most is reached.
All inputs are finite; a program needn't handle non-finite values.
Results may differ from the reference program's by a relative error of at most 0.023.
Values may be sent and summed in bfloat16 or wider, within the bound.
No kernel may reach another device: no remote copies, remote signals or barrier semaphores. Data moves between devices by JAX's collectives and lax.ppermute only.
A program may use at most 128 MiB of HBM per device.

```python
import math
import jax
import jax.numpy as jnp
import numpy as np
from jax import lax

D = 6144
HEADS = 64
HD = 128
FF = 4608
TOPK = 2
BLOCK = 128
WINDOW_TOKENS = 2048
EXPERTS = 8
TOKS = 16
CAP = 8
N_SEQ = 16
N_EXP = 8


def draw_log_decay(key, part):
    key = jax.random.fold_in(key, 11)
    rate_random_key, noise_random_key, spike_random_key, depth_random_key = jax.random.split(key, 4)
    low, high = (0.02 / WINDOW_TOKENS, 0.05)
    per_head_rate = jnp.exp(jax.random.uniform(rate_random_key, (HEADS, 1), jnp.float32, jnp.log(low), jnp.log(high)))
    random_noise = jnp.exp(jax.random.uniform(noise_random_key, (HEADS, WINDOW_TOKENS), jnp.float32, -0.7, 0.7))
    spike_amount = (jax.random.randint(spike_random_key, (1, WINDOW_TOKENS), 0, WINDOW_TOKENS) < 2).astype(jnp.float32)
    stack_depth = jax.random.uniform(depth_random_key, (HEADS, WINDOW_TOKENS), jnp.float32, 0.22, 0.69)
    return -(per_head_rate * random_noise) - spike_amount * stack_depth


def block_scale(key, shape, pieces, smallest, largest):
    factor_of, own = 1.0, jax.random.fold_in(key, 6)
    for axis_at, blocks in pieces:
        heights = jnp.exp(jax.random.uniform(jax.random.fold_in(own, axis_at), (blocks,), jnp.float32, smallest / len(pieces), largest / len(pieces)))
        factor_of = factor_of * jnp.repeat(heights, shape[axis_at] // blocks).reshape([-1 if axis == axis_at else 1 for axis in range(len(shape))])
    return factor_of


def shared_out(stream_key, own, number, rows, count, top, limit, skew):
    ranking = jax.random.permutation(stream_key, count)
    heavy_load, usual = shares(count, rows * top, limit, skew, True), shares(count, rows * top, limit, skew, False)
    places = jnp.arange(count)

    def named(lengths, turn):
        used = int((lengths > 0).sum())
        fixed = max(1, used // 4)
        moved = fixed + (places - fixed + turn * (used - fixed)) % max(1, count - fixed)
        return jnp.zeros((count,), jnp.int32).at[ranking[jnp.where(places < fixed, places, moved)]].set(jnp.asarray(lengths, jnp.int32))

    lengths = jnp.where(number % 4 == 0, named(heavy_load, number // 4), named(usual, number - number // 4 - 1))
    mixed = jax.random.permutation(jax.random.fold_in(own, 3), count)
    source_of, taker = mixed[0:count // 2 * 2:2], mixed[1:count // 2 * 2:2]
    margin = jnp.minimum(lengths[source_of] - 1, limit - lengths[taker]) // 2
    margin = jnp.where((source_of == ranking[0]) | (taker == ranking[0]) | (lengths[taker] == 0), 0, jnp.maximum(margin, 0))
    moved = jax.random.randint(jax.random.fold_in(own, 4), (count // 2,), 0, 1 << 20) % (margin + 1)
    lengths = lengths.at[source_of].add(-moved).at[taker].add(moved)
    items = jnp.searchsorted(jnp.cumsum(lengths), jnp.arange(rows * top), side="right").astype(jnp.int32)
    grid = items.reshape(top, rows).T
    grid = grid[jax.random.permutation(jax.random.fold_in(own, 1), rows)]
    turn = jax.random.randint(jax.random.fold_in(own, 2), (rows, 1), 0, top)
    return jnp.take_along_axis(grid, (jnp.arange(top)[None, :] + turn) % top, axis=1)


def shares(count, total, most, lean, full):
    portions = [(1 << 20) // math.isqrt(rank ** lean) + 1 for rank in range(1, count + 1)]
    largest = most if full else min(most, max(-(-total // count), total * portions[0] // sum(portions)))
    least = 1 if total - largest >= count - 1 else 0
    holding, surplus = [largest] + [least] * (count - 1), total - largest - least * (count - 1)
    while surplus > 0:
        free = [i for i in range(1, count) if holding[i] < largest] or [i for i in range(1, count) if holding[i] < most]
        pool, budget = sum([portions[i] for i in free]), surplus
        for i in free:
            addition = min(most - holding[i], max(1, budget * portions[i] // pool), surplus)
            holding[i] = holding[i] + addition
            surplus = surplus - addition
    return np.array(holding)


def centred(rng, extent, width, bound, shards=(), kind=jnp.bfloat16):
    array = jax.random.normal(rng, extent, jnp.float32) * width
    if len(shards) > 0:
        array = block_scale(rng, extent, shards, -0.22, 0.18) * array
    return jnp.clip(array, min=-bound, max=bound).astype(kind)


def setup_inputs(seed: int = 0) -> dict:
    splits = jax.random.split(jax.random.key(seed), 15)
    hidden_in = centred(splits[0], (WINDOW_TOKENS, D), 1.0, 6.0, ((0, 128),))
    queries = centred(splits[1], (WINDOW_TOKENS, HEADS * HD), 0.5, 4.0, ((0, 16), (1, 8)))
    key_rows = centred(splits[2], (WINDOW_TOKENS, HEADS * HD), 0.5, 4.0, ((0, 16), (1, 8)))
    value_rows = centred(splits[3], (WINDOW_TOKENS, HEADS * HD), 1.0, 6.0, ((0, 16), (1, 8)))
    out_gate = centred(splits[4], (WINDOW_TOKENS, HEADS * HD), 1.0, 6.0, ((0, 16), (1, 8)))
    log_decay = draw_log_decay(jax.random.fold_in(splits[14], 71), 0)
    attn_gain = jnp.clip(1.0 + 0.15 * jax.random.normal(splits[6], (HEADS * HD,), jnp.float32), 0.25, 1.75)
    out_weight = centred(splits[7], (HEADS * HD, D), (HEADS * HD) ** -0.5, 0.0625, ((0, 8),))
    ffn_gain = jnp.clip(1.0 + 0.15 * jax.random.normal(splits[8], (D,), jnp.float32), 0.25, 1.75)
    routes_keys = jax.random.split(jax.random.fold_in(splits[9], 1), WINDOW_TOKENS // TOKS)
    routes_turns = jax.random.permutation(jax.random.fold_in(splits[9], 3), WINDOW_TOKENS // TOKS)
    routes = jax.vmap(lambda own, number: shared_out(jax.random.fold_in(splits[9], 2), own, number, TOKS, EXPERTS, TOPK, CAP, 2))(routes_keys, routes_turns).reshape((WINDOW_TOKENS, TOPK))
    combine_weight = jnp.clip(0.2 + 0.8 * jax.random.uniform(splits[10], (WINDOW_TOKENS, TOPK), jnp.float32) ** block_scale(splits[10], (WINDOW_TOKENS, TOPK), ((0, 128),), -0.2, 0.2), 0.2, 1.0)
    gate_weight = centred(splits[11], (EXPERTS, D, FF), D ** -0.5, 0.078125, ((0, 8), (2, 16)))
    up_weight = centred(splits[12], (EXPERTS, D, FF), D ** -0.5, 0.078125, ((0, 8), (2, 16)))
    down_weight = centred(splits[13], (EXPERTS, FF, D), FF ** -0.5, 0.09375, ((0, 8), (1, 16)))
    return {"hidden_in": hidden_in, "queries": queries, "key_rows": key_rows, "value_rows": value_rows, "out_gate": out_gate, "log_decay": log_decay, "attn_gain": attn_gain, "out_weight": out_weight, "ffn_gain": ffn_gain, "routes": routes, "combine_weight": combine_weight, "gate_weight": gate_weight, "up_weight": up_weight, "down_weight": down_weight}


def reference(hidden_in, queries, key_rows, value_rows, out_gate, log_decay, attn_gain, out_weight, ffn_gain, routes, combine_weight, gate_weight, up_weight, down_weight):
    f32 = jnp.float32
    q_heads = queries.reshape(N_SEQ, BLOCK, HEADS, HD).astype(f32)
    k_heads = key_rows.reshape(N_SEQ, BLOCK, HEADS, HD).astype(f32)
    v_heads = value_rows.reshape(N_SEQ, BLOCK, HEADS, HD).astype(f32)
    cum = jnp.cumsum(log_decay.reshape(HEADS, N_SEQ, BLOCK), axis=2).transpose(1, 0, 2)
    ends = cum[:, :, -1]
    scores = jnp.einsum('nthd,nshd->nhts', q_heads, k_heads)
    causal = jnp.arange(BLOCK)[:, None] >= jnp.arange(BLOCK)[None, :]
    spread = cum[:, :, :, None] - cum[:, :, None, :]
    weights = jnp.where(causal, scores * jnp.exp(jnp.where(causal, spread, 0.0)), 0.0).astype(jnp.bfloat16)
    intra = jnp.einsum('nhts,nshd->nthd', weights.astype(f32), v_heads)
    factor = jnp.exp(ends[:, :, None] - cum).transpose(0, 2, 1)
    keyed = (k_heads * factor[..., None]).astype(jnp.bfloat16)
    state = jnp.einsum('nshd,nshe->nhde', keyed.astype(f32), v_heads)

    def advance(carry, items):
        total, block_state = items
        return (jnp.exp(total)[:, None, None] * carry + block_state, carry)
    _, incoming = lax.scan(advance, jnp.zeros((HEADS, HD, HD), f32), (ends, state))
    scaled_q = q_heads * jnp.exp(cum).transpose(0, 2, 1)[..., None]
    inter = jnp.einsum('nthd,nhde->nthe', scaled_q, incoming, precision=lax.Precision.HIGHEST)
    mixed_heads = intra + inter
    gain_heads = attn_gain.reshape(HEADS, HD)
    normal_heads = mixed_heads * lax.rsqrt(lax.optimization_barrier(jnp.mean(mixed_heads * mixed_heads, axis=-1, keepdims=True)) + 1e-05)
    gate_heads = jax.nn.sigmoid(out_gate.reshape(N_SEQ, BLOCK, HEADS, HD).astype(f32))
    gated = (normal_heads * gain_heads * gate_heads).astype(jnp.bfloat16).reshape(WINDOW_TOKENS, HEADS * HD)
    mid = (hidden_in.astype(f32) + jnp.dot(gated, out_weight, preferred_element_type=f32)).astype(jnp.bfloat16)
    mid_f = mid.astype(f32)
    normed = (mid_f * lax.rsqrt(lax.optimization_barrier(jnp.mean(mid_f * mid_f, axis=-1, keepdims=True)) + 1e-06) * ffn_gain).astype(jnp.bfloat16)
    devs = N_SEQ * N_EXP
    pairs = 2 * TOKS
    flat = routes.reshape(devs, pairs).astype(jnp.int32)
    onehot = (flat[:, :, None] == jnp.arange(EXPERTS, dtype=jnp.int32)[None, None, :]).astype(jnp.int32)
    earlier = jnp.cumsum(onehot, axis=1) - onehot
    slot = lax.optimization_barrier(jnp.sum(earlier * onehot, axis=-1)).astype(jnp.int32)
    device_ids = jnp.arange(devs, dtype=jnp.int32)[:, None]
    position = (device_ids * CAP + slot).astype(jnp.int32)
    token_ids = (device_ids * TOKS + jnp.arange(pairs, dtype=jnp.int32)[None, :] // 2).astype(jnp.int32)
    table = jnp.full((EXPERTS, devs * CAP), WINDOW_TOKENS, jnp.int32).at[flat, position].set(token_ids)
    padded = jnp.concatenate([normed, jnp.zeros((1, D), jnp.bfloat16)], axis=0)
    slice_size = FF // N_SEQ

    def run_expert(items):
        w_gate, w_up, w_down, row_ids = items
        rows = padded[row_ids]
        total = jnp.zeros((devs * CAP, D), f32)
        for part_no in range(N_SEQ):
            lower = part_no * slice_size
            gate_part = jnp.dot(rows, w_gate[:, lower:lower + slice_size], preferred_element_type=f32)
            up_part = jnp.dot(rows, w_up[:, lower:lower + slice_size], preferred_element_type=f32)
            hidden = (jax.nn.silu(gate_part) * up_part).astype(jnp.bfloat16)
            partial_sum = jnp.dot(hidden, w_down[lower:lower + slice_size, :], preferred_element_type=f32)
            total = total + lax.optimization_barrier(partial_sum.astype(jnp.bfloat16)).astype(f32)
        return total.astype(jnp.bfloat16)
    expert_out = lax.map(run_expert, (gate_weight, up_weight, down_weight, table))
    picked = expert_out[flat, position].reshape(WINDOW_TOKENS, 2, D).astype(f32)
    weighted = lax.optimization_barrier(jnp.sum(picked * combine_weight[:, :, None], axis=1))
    return (mid_f + weighted).astype(jnp.bfloat16)
```

```python
import functools

import jax
import jax.numpy as jnp
from jax import lax
from jax.experimental import pallas as pl
from jax.experimental.pallas import tpu as pltpu
from jax.sharding import PartitionSpec as P

f32 = jnp.float32
bf16 = jnp.bfloat16
SIDE = 4
CORES = 2
AXES = ("seq", "exp")
HD = 128
VMEM_LIMIT = 48 * 1024 * 1024


def permutation(move):
    pairs = []
    for z in range(SIDE):
        for y in range(SIDE):
            for x in range(SIDE):
                for c in range(CORES):
                    z2, y2, x2, c2 = move(z, y, x, c)
                    source = ((z * SIDE + y) * SIDE + x) * CORES + c
                    target = (((z2 % SIDE) * SIDE + y2 % SIDE) * SIDE + x2 % SIDE) * CORES + c2
                    pairs.append((source, target))
    return pairs


def along_x(k):
    return permutation(lambda z, y, x, c: (z, y, x + k, c))


def along_first(k):
    return permutation(lambda z, y, x, c: (z, y + k, x, c) if c == 0 else (z + k, y, x, c))


def along_second(k):
    return permutation(lambda z, y, x, c: (z + k, y, x, c) if c == 0 else (z, y + k, x, c))


OTHER_CORE = permutation(lambda z, y, x, c: (z, y, x, 1 - c))


def send(value, perm):
    return lax.ppermute(value, AXES, perm)


def split3(value):
    high = lax.reduce_precision(value, 8, 7)
    rest = value - high
    mid = lax.reduce_precision(rest, 8, 7)
    return high, mid, rest - mid


def lower_triangle(n):
    row = lax.broadcasted_iota(jnp.int32, (n, n), 0)
    col = lax.broadcasted_iota(jnp.int32, (n, n), 1)
    return row >= col


def dot_nt(a, b, **kw):
    return lax.dot_general(a, b, (((1,), (1,)), ((), ())), preferred_element_type=f32, **kw)


def dot_tn(a, b, **kw):
    return lax.dot_general(a, b, (((0,), (0,)), ((), ())), preferred_element_type=f32, **kw)


def state_kernel(k_ref, v_ref, ld_ref, out_ref):
    heads, block = ld_ref.shape
    low = lower_triangle(block).astype(f32)
    ld = ld_ref[...]
    cum_col = dot_nt(low, ld, precision=lax.Precision.HIGHEST)
    ends = cum_col[block - 1 : block, :]
    factor = jnp.exp(ends - cum_col)
    rows = lax.broadcasted_iota(jnp.int32, (16, HD), 0)
    for h in range(heads):
        lanes = pl.ds(h * HD, HD)
        keyed = (k_ref[:, lanes].astype(f32) * factor[:, h : h + 1]).astype(bf16)
        state = dot_tn(keyed, v_ref[:, lanes]).astype(bf16)
        end = jnp.broadcast_to(ends[:, h : h + 1], (16, HD))
        high = end.astype(bf16).astype(f32)
        rest = end - high
        mid = rest.astype(bf16).astype(f32)
        tail = jnp.where(rows == 0, high, jnp.where(rows == 1, mid, jnp.where(rows == 2, rest - mid, 0.0)))
        tail = tail.astype(bf16)
        for part in range(2):
            out_ref[2 * h + part, 0:64, :] = state[part * 64 : part * 64 + 64]
            out_ref[2 * h + part, 64:80, :] = tail


def scan_kernel(in_ref, out_ref):
    count = in_ref.shape[0]
    carry = jnp.zeros((64, HD), f32)
    for i in range(count):
        out_ref[i] = carry.astype(bf16)
        if i + 1 < count:
            tail = in_ref[i, 64:80, :].astype(f32)
            end = tail[0:1] + tail[1:2] + tail[2:3]
            carry = jnp.exp(end) * carry + in_ref[i, 0:64, :].astype(f32)


def mix_kernel(place, q_ref, k_ref, v_ref, g_ref, ld_ref, inc_ref, gain_ref, w_ref, out_ref, gated):
    heads, block = ld_ref.shape
    core = place[1]

    @pl.when(pl.program_id(0) == 0)
    def _():
        causal = lower_triangle(block)
        low = causal.astype(f32)
        ld = ld_ref[...]
        cum_col = dot_nt(low, ld, precision=lax.Precision.HIGHEST)
        cum_row = dot_nt(ld, low, precision=lax.Precision.HIGHEST)
        grown = jnp.exp(cum_col)
        for h in range(heads):
            lanes = pl.ds(h * HD, HD)
            q, k, v = q_ref[:, lanes], k_ref[:, lanes], v_ref[:, lanes]
            spread = cum_col[:, h : h + 1] - cum_row[h : h + 1, :]
            weights = jnp.where(causal, dot_nt(q, k) * jnp.exp(jnp.where(causal, spread, 0.0)), 0.0)
            intra = jnp.dot(weights.astype(bf16), v, preferred_element_type=f32)
            inter = jnp.dot(q, inc_ref[h], preferred_element_type=f32) * grown[:, h : h + 1]
            mixed = intra + inter
            normal = mixed * lax.rsqrt(jnp.mean(mixed * mixed, axis=-1, keepdims=True) + 1e-05)
            gate = 1.0 / (1.0 + jnp.exp(-g_ref[:, lanes].astype(f32)))
            result = (normal * gain_ref[:, lanes] * gate).astype(bf16)
            for x in range(SIDE):
                for c in range(CORES):
                    there, here = c * 64 + x * 16, x * 32 + c * 16
                    gated[there : there + 16, lanes] = result[here : here + 16]

    product = jnp.dot(gated[...], w_ref[...], preferred_element_type=f32).astype(bf16)
    out_ref[core, 0] = product[:64]
    out_ref[1 - core, 0] = product[64:]


def attention(place, queries, key_rows, value_rows, out_gate, log_decay, attn_gain, out_weight):
    heads = log_decay.shape[0]
    block = queries.shape[0]
    width = out_weight.shape[1]
    pieces = pl.pallas_call(
        state_kernel,
        out_shape=jax.ShapeDtypeStruct((2 * heads, 80, HD), bf16),
        compiler_params=pltpu.CompilerParams(vmem_limit_bytes=VMEM_LIMIT),
    )(key_rows, value_rows, log_decay)
    pieces = lax.all_to_all(pieces, "seq", split_axis=0, concat_axis=0, tiled=True)
    before = pl.pallas_call(
        scan_kernel,
        out_shape=jax.ShapeDtypeStruct((2 * heads, 64, HD), bf16),
        compiler_params=pltpu.CompilerParams(vmem_limit_bytes=VMEM_LIMIT),
    )(pieces)
    before = lax.all_to_all(before, "seq", split_axis=0, concat_axis=0, tiled=True)
    incoming = before.reshape(heads, HD, HD)
    tile = 512
    per = width // SIDE // tile
    whole = lambda *shape: pl.BlockSpec(shape, lambda j, p: (0,) * len(shape))
    return pl.pallas_call(
        mix_kernel,
        grid_spec=pltpu.PrefetchScalarGridSpec(
            num_scalar_prefetch=1,
            grid=(width // tile,),
            in_specs=[whole(block, heads * HD)] * 4
            + [
                whole(heads, block),
                whole(heads, HD, HD),
                whole(1, heads * HD),
                pl.BlockSpec((heads * HD, tile), lambda j, p: (0, j)),
            ],
            out_specs=pl.BlockSpec(
                (2, 1, 64, tile), lambda j, p: (0, lax.rem(j // per + SIDE - p[0], SIDE), 0, lax.rem(j, per))
            ),
            scratch_shapes=[pltpu.VMEM((block, heads * HD), bf16)],
        ),
        out_shape=jax.ShapeDtypeStruct((CORES, SIDE, 64, width // SIDE), bf16),
        compiler_params=pltpu.CompilerParams(vmem_limit_bytes=VMEM_LIMIT),
    )(place, queries, key_rows, value_rows, out_gate, log_decay, incoming, attn_gain.reshape(1, -1), out_weight)


def gate_up_kernel(groups, ids, *refs):
    x_refs, (own_ref, swap_ref, out_ref, acc) = refs[:-4], refs[-4:]
    step = pl.program_id(0)
    depth = own_ref.shape[2]
    wide = own_ref.shape[1]
    blocks = [(ref, i) for ref in x_refs for i in range(ref.shape[0])]
    rows = len(blocks) * 64
    x = jnp.concatenate([ref[...].reshape(-1, ref.shape[2])[:, :depth] for ref in x_refs], 0)
    meta = jnp.concatenate([ref[...].reshape(-1, ref.shape[2])[:, depth:] for ref in x_refs], 0)
    first = meta[:, 64:65].astype(f32)
    second = meta[:, 65:66].astype(f32)
    for which, w_ref in ((0, own_ref), (1, swap_ref)):
        expert = ids[2 + which * 4 + step].astype(f32)
        part = dot_nt(x, w_ref[0])
        acc[0, :, :wide] = jnp.where(first == expert, part, acc[0, :, :wide])
        acc[1, :, :wide] = jnp.where(second == expert, part, acc[1, :, :wide])

    @pl.when(step == pl.num_programs(0) - 1)
    def _():
        lane = lax.broadcasted_iota(jnp.int32, (rows, 128), 1)
        edge = wide // 128 * 128
        for k in range(2):
            last = jnp.where(lane < 64, acc[k, :, edge : edge + 128], meta.astype(f32)).astype(bf16)
            head = acc[k, :, :edge].astype(bf16)
            for i in range(len(blocks)):
                rel = lax.rem(i % 4 + SIDE - ids[0], SIDE)
                at = k * (edge + 128)
                out_ref[rel, i // 4, :, at : at + edge] = head[i * 64 : i * 64 + 64]
                out_ref[rel, i // 4, :, at + edge : at + edge + 128] = last[i * 64 : i * 64 + 64]


def gate_up(ids, xs, own, swap):
    count = sum(x.shape[0] for x in xs)
    groups = count // SIDE
    wide = own.shape[1]
    padded = wide // 128 * 128 + 128
    whole = lambda shape: pl.BlockSpec(shape, lambda j, p: (0,) * len(shape))
    shape = (SIDE, groups, 64, 2 * padded)
    return pl.pallas_call(
        functools.partial(gate_up_kernel, groups),
        grid_spec=pltpu.PrefetchScalarGridSpec(
            num_scalar_prefetch=1,
            grid=(SIDE,),
            in_specs=[whole(x.shape) for x in xs]
            + [pl.BlockSpec((1,) + own.shape[1:], lambda j, p: (j, 0, 0))] * 2,
            out_specs=whole(shape),
            scratch_shapes=[pltpu.VMEM((2, count * 64, padded), f32)],
        ),
        out_shape=jax.ShapeDtypeStruct(shape, bf16),
        compiler_params=pltpu.CompilerParams(vmem_limit_bytes=VMEM_LIMIT),
    )(ids, *xs, own, swap)


def down_kernel(ids, h_ref, own_ref, swap_ref, out_ref, spread):
    rows = h_ref.shape[1] * 64
    h = h_ref[0].reshape(rows, h_ref.shape[3]).astype(f32)
    pad = own_ref.shape[1]
    first = h[:, 288:289]
    second = h[:, 289:290]
    for which in range(2):
        for j in range(SIDE):
            expert = ids[2 + which * 4 + j].astype(f32)
            kept = jnp.where(first == expert, h[:, :pad], 0.0) + jnp.where(second == expert, h[:, pad:], 0.0)
            spread[:, (which * 4 + j) * pad : (which * 4 + j + 1) * pad] = kept.astype(bf16)
    half = SIDE * pad
    result = jnp.dot(spread[:, :half], own_ref[...].reshape(half, -1), preferred_element_type=f32)
    result += jnp.dot(spread[:, half:], swap_ref[...].reshape(half, -1), preferred_element_type=f32)
    out_ref[...] = result.astype(bf16).reshape(out_ref.shape)


def down(ids, hidden, own, swap):
    width = own.shape[2]
    shape = (SIDE, SIDE, 64, width)
    whole = lambda shape: pl.BlockSpec(shape, lambda j, p: (0,) * len(shape))
    return pl.pallas_call(
        down_kernel,
        grid_spec=pltpu.PrefetchScalarGridSpec(
            num_scalar_prefetch=1,
            grid=(SIDE,),
            in_specs=[
                pl.BlockSpec((1,) + hidden.shape[1:], lambda j, p: (j, 0, 0, 0)),
                whole(own.shape),
                whole(swap.shape),
            ],
            out_specs=pl.BlockSpec((SIDE, 1, 64, width), lambda j, p: (0, p[10 + j], 0, 0)),
            scratch_shapes=[pltpu.VMEM((hidden.shape[1] * 64, 8 * own.shape[1]), bf16)],
        ),
        out_shape=jax.ShapeDtypeStruct(shape, bf16),
        compiler_params=pltpu.CompilerParams(vmem_limit_bytes=VMEM_LIMIT),
    )(ids, hidden, own, swap)


def ring_gather(value, perm):
    half = value.shape[0] // 2
    right = send(value, perm(1))
    left = send(value, perm(-1))
    far = (send(right[:half], perm(1)), send(left[half:], perm(-1)))
    return right, left, far


def plus(a, b):
    return (a.astype(f32) + b.astype(f32)).astype(bf16)


def ring_reduce(own, behind, ahead, far, perm):
    half = far.shape[0] // 2
    from_behind = send(far[:half], perm(1))
    from_ahead = send(far[half:], perm(-1))
    to_ahead = jnp.concatenate([plus(ahead[:half], from_behind), ahead[half:]], 0)
    to_behind = jnp.concatenate([behind[:half], plus(behind[half:], from_ahead)], 0)
    got = send(to_ahead, perm(1)), send(to_behind, perm(-1))
    return own.astype(f32) + got[0].astype(f32) + got[1].astype(f32)


def per_device(
    hidden_in,
    queries,
    key_rows,
    value_rows,
    out_gate,
    log_decay,
    attn_gain,
    out_weight,
    ffn_gain,
    routes,
    combine_weight,
    gate_weight,
    up_weight,
    down_weight,
):
    width = hidden_in.shape[1]
    part = width // SIDE
    units = gate_weight.shape[2]
    at = lax.axis_index("exp")
    x, core = at // CORES, lax.rem(at, CORES)
    order = [0, -1, 1, 2]
    chips = [lax.rem(x + d + SIDE, SIDE) for d in order]
    place = jnp.stack(
        [x, core]
        + [2 * chip + core for chip in chips]
        + [2 * chip + 1 - core for chip in chips]
        + chips
    ).astype(jnp.int32)

    gate_t, up_t, down_w = gate_weight[0].T, up_weight[0].T, down_weight[0]

    def piece(d):
        start = lax.rem(x + d + SIDE, SIDE) * part
        cut = lambda w: lax.dynamic_slice(w, (0, start), (units, part))
        return jnp.concatenate([cut(gate_t), cut(up_t)], 0), cut(down_w)

    mine, ahead, behind, far = piece(0), piece(1), piece(-1), piece(2)
    gu = [mine[0], send(ahead[0], along_x(1)), send(behind[0], along_x(-1)), send(far[0], along_x(2))]
    gu_own = jnp.stack(gu)
    gu_swap = send(gu_own, OTHER_CORE)
    dn = [mine[1], send(ahead[1], along_x(1)), send(behind[1], along_x(-1)), send(far[1], along_x(2))]
    pad = -units % 128
    dn_own = jnp.stack([jnp.pad(d, ((0, pad), (0, 0))) for d in dn])
    dn_swap = send(dn_own, OTHER_CORE)

    toks = hidden_in.shape[0]
    routes_f = routes.astype(f32)
    cw = split3(combine_weight)
    lanes = [routes_f[:, 0:1], routes_f[:, 1:2]] + [w[:, k : k + 1] for k in range(2) for w in cw]
    meta = jnp.concatenate([jnp.zeros((toks, 64), f32)] + lanes + [jnp.zeros((toks, 64 - len(lanes)), f32)], 1)
    stacked = jnp.concatenate(
        [
            hidden_in.reshape(toks, SIDE, part).transpose(1, 0, 2),
            jnp.broadcast_to(meta.astype(bf16)[None], (SIDE, toks, 128)),
        ],
        2,
    )
    groups = [[2 * i + c + 8 * s for i in range(SIDE)] for s in range(16) for c in range(CORES)]
    here = lax.all_to_all(
        stacked, "exp", split_axis=0, concat_axis=0, tiled=True,
        axis_index_groups=[[2 * i + c for i in range(SIDE)] for c in range(CORES)],
    ).reshape(SIDE * toks, part + 128)

    partial = attention(place, queries, key_rows, value_rows, out_gate, log_decay, attn_gain, out_weight)
    summed = plus(partial[0], send(partial[1], OTHER_CORE))
    got = [send(summed[1], along_x(1)), send(summed[3], along_x(-1)), send(summed[2], along_x(2))]
    mixed = summed[0].astype(f32)
    for g in got:
        mixed = mixed + g.astype(f32)
    mid = (here[:, :part].astype(f32) + mixed).astype(bf16)
    mid_f = mid.astype(f32)
    gain = lax.dynamic_slice(ffn_gain, (x * part,), (part,))
    squares = split3(jnp.sum(mid_f * mid_f, axis=1, keepdims=True))
    tail = here[:, part:]
    tail = jnp.concatenate([tail[:, :72], squares[0].astype(bf16), squares[1].astype(bf16), tail[:, 74:]], 1)
    rows = jnp.concatenate([(mid_f * gain).astype(bf16), tail], 1)

    right, left, far = ring_gather(rows, along_first)
    plane = jnp.stack([rows, right, left, jnp.concatenate(far, 0)])
    right, left, far = ring_gather(plane, along_second)
    y_near = gate_up(place, [plane], gu_own, gu_swap)
    y_far = gate_up(place, [right, left, far[0], far[1]], gu_own, gu_swap)
    y = jnp.concatenate([y_near, y_far], 1)
    z = ring_reduce(y[0], y[3], y[1], y[2], along_x)

    wide = 2 * units
    col = z.shape[2] // 2
    scale = lax.rsqrt((z[:, :, wide + 8 : wide + 9] + z[:, :, wide + 9 : wide + 10]) / width + 1e-06)
    hidden = []
    for k in range(2):
        gate = z[:, :, k * col : k * col + units] * scale
        up = z[:, :, k * col + units : k * col + wide] * scale
        lane = wide + 2 + 3 * k
        weight = jnp.sum(z[:, :, lane : lane + 3], axis=2, keepdims=True) * (1.0 / SIDE)
        value = jax.nn.silu(gate) * up * weight
        extra = z[:, :, wide : wide + 2] * (1.0 / SIDE)
        hidden += [value, extra, jnp.zeros(value.shape[:2] + (pad - 2,), f32)]
    hidden = jnp.concatenate(hidden, 2).astype(bf16)
    right, left, far = ring_gather(hidden, along_x)
    hidden = jnp.stack([hidden, right, left, jnp.concatenate(far, 0)])
    out = down(place, hidden, dn_own, dn_swap)
    out = ring_reduce(out[0], out[1], out[2], out[3], along_second).astype(bf16)
    out = ring_reduce(out[0], out[1], out[2], out[3], along_first)
    out = (mid_f + out).astype(bf16).reshape(SIDE, toks, part)
    out = lax.all_to_all(
        out, "exp", split_axis=0, concat_axis=0, tiled=True,
        axis_index_groups=[[2 * i + c for i in range(SIDE)] for c in range(CORES)],
    )
    return out.transpose(1, 0, 2).reshape(toks, width)


def solution(mesh):
    return jax.shard_map(
        per_device,
        mesh=mesh,
        in_specs=(
            P(("seq", "exp"), None),
            P("seq", "exp"),
            P("seq", "exp"),
            P("seq", "exp"),
            P("seq", "exp"),
            P("exp", "seq"),
            P("exp"),
            P("exp", None),
            P(),
            P(("seq", "exp"), None),
            P(("seq", "exp"), None),
            P("exp", None, "seq"),
            P("exp", None, "seq"),
            P("exp", "seq", None),
        ),
        out_specs=P(("seq", "exp"), None),
        check_vma=False,
    )
```

```python
import functools

import jax
import jax.numpy as jnp
from jax import lax
from jax.experimental import pallas as pl
from jax.experimental.pallas import tpu as pltpu
from jax.sharding import PartitionSpec as P

f32 = jnp.float32
bf16 = jnp.bfloat16
SIDE = 4
CORES = 2
AXES = ("seq", "exp")
HD = 128


def permutation(move):
    pairs = []
    for z in range(SIDE):
        for y in range(SIDE):
            for x in range(SIDE):
                for c in range(CORES):
                    z2, y2, x2, c2 = move(z, y, x, c)
                    source = ((z * SIDE + y) * SIDE + x) * CORES + c
                    target = (((z2 % SIDE) * SIDE + y2 % SIDE) * SIDE + x2 % SIDE) * CORES + c2
                    pairs.append((source, target))
    return pairs


def along_x(k):
    return permutation(lambda z, y, x, c: (z, y, x + k, c))


def along_first(k):
    return permutation(lambda z, y, x, c: (z, y + k, x, c) if c == 0 else (z + k, y, x, c))


def along_second(k):
    return permutation(lambda z, y, x, c: (z + k, y, x, c) if c == 0 else (z, y + k, x, c))


OTHER_CORE = permutation(lambda z, y, x, c: (z, y, x, 1 - c))


def send(value, perm):
    return lax.ppermute(value, AXES, perm)


def split3(value):
    high = lax.reduce_precision(value, 8, 7)
    rest = value - high
    mid = lax.reduce_precision(rest, 8, 7)
    return high, mid, rest - mid


def lower_triangle(n):
    row = lax.broadcasted_iota(jnp.int32, (n, n), 0)
    col = lax.broadcasted_iota(jnp.int32, (n, n), 1)
    return row >= col


def dot_nt(a, b, **kw):
    return lax.dot_general(a, b, (((1,), (1,)), ((), ())), preferred_element_type=f32, **kw)


def dot_tn(a, b, **kw):
    return lax.dot_general(a, b, (((0,), (0,)), ((), ())), preferred_element_type=f32, **kw)


def state_kernel(k_ref, v_ref, ld_ref, out_ref):
    heads, block = ld_ref.shape
    low = lower_triangle(block).astype(f32)
    ld = ld_ref[...]
    cum_col = dot_nt(low, ld, precision=lax.Precision.HIGHEST)
    ends = cum_col[block - 1 : block, :]
    factor = jnp.exp(ends - cum_col)
    rows = lax.broadcasted_iota(jnp.int32, (16, HD), 0)
    for h in range(heads):
        lanes = pl.ds(h * HD, HD)
        keyed = (k_ref[:, lanes].astype(f32) * factor[:, h : h + 1]).astype(bf16)
        state = dot_tn(keyed, v_ref[:, lanes]).astype(bf16)
        end = jnp.broadcast_to(ends[:, h : h + 1], (16, HD))
        high = end.astype(bf16).astype(f32)
        rest = end - high
        mid = rest.astype(bf16).astype(f32)
        tail = jnp.where(rows == 0, high, jnp.where(rows == 1, mid, jnp.where(rows == 2, rest - mid, 0.0)))
        tail = tail.astype(bf16)
        for part in range(2):
            out_ref[2 * h + part, 0:64, :] = state[part * 64 : part * 64 + 64]
            out_ref[2 * h + part, 64:80, :] = tail


def scan_kernel(in_ref, out_ref):
    count = in_ref.shape[0]
    carry = jnp.zeros((64, HD), f32)
    for i in range(count):
        out_ref[i] = carry.astype(bf16)
        if i + 1 < count:
            tail = in_ref[i, 64:80, :].astype(f32)
            end = tail[0:1] + tail[1:2] + tail[2:3]
            carry = jnp.exp(end) * carry + in_ref[i, 0:64, :].astype(f32)


def mix_kernel(
    place, q_ref, k_ref, v_ref, g_ref, ld_ref, inc_ref, gain_ref, hid_ref, meta_ref, w_ref,
    mine_ref, other_ref, gated, buffer, sems,
):
    heads, block = ld_ref.shape
    tiles = buffer.shape[0]
    tile = buffer.shape[2]
    copies = [
        pltpu.make_async_copy(w_ref.at[:, pl.ds(i * tile, tile)], buffer.at[i], sems.at[i]) for i in range(tiles)
    ]
    for copy in copies:
        copy.start()
    causal = lower_triangle(block)
    low = causal.astype(f32)
    ld = ld_ref[...]
    cum_col = dot_nt(low, ld, precision=lax.Precision.HIGHEST)
    cum_row = dot_nt(ld, low, precision=lax.Precision.HIGHEST)
    grown = jnp.exp(cum_col)
    for h in range(heads):
        lanes = pl.ds(h * HD, HD)
        q, k, v = q_ref[:, lanes], k_ref[:, lanes], v_ref[:, lanes]
        spread = cum_col[:, h : h + 1] - cum_row[h : h + 1, :]
        weights = jnp.where(causal, dot_nt(q, k) * jnp.exp(jnp.where(causal, spread, 0.0)), 0.0)
        intra = jnp.dot(weights.astype(bf16), v, preferred_element_type=f32)
        inter = jnp.dot(q, inc_ref[h], preferred_element_type=f32) * grown[:, h : h + 1]
        mixed = intra + inter
        normal = mixed * lax.rsqrt(jnp.mean(mixed * mixed, axis=-1, keepdims=True) + 1e-05)
        gate = 1.0 / (1.0 + jnp.exp(-g_ref[:, lanes].astype(f32)))
        result = (normal * gain_ref[:, lanes] * gate).astype(bf16)
        for x in range(SIDE):
            for c in range(CORES):
                there, here = c * 64 + x * 16, x * 32 + c * 16
                gated[there : there + 16, lanes] = result[here : here + 16]
    core = place[1]
    toks = hid_ref.shape[0]
    own = pl.ds(pl.multiple_of(place[0] * toks, toks), toks)
    half = lambda c: pl.ds(pl.multiple_of(c * 64, 64), 64)
    per = tiles // SIDE
    width = per * tile
    for rel in range(SIDE):
        mine_ref[rel, :, width:] = jnp.zeros((64, 128), bf16)
        mine_ref[rel, own, width:] = meta_ref[...]
    for i in range(tiles):
        copies[i].wait()
        rel = lax.rem(i // per + SIDE - place[0], SIDE)
        lanes = pl.ds(i % per * tile, tile)
        rows = gated[half(core)]
        product = jnp.dot(rows, buffer[i], preferred_element_type=f32)
        mine_ref[rel, :, lanes] = product.astype(bf16)
        again = mine_ref[rel, own, lanes].astype(f32) + hid_ref[:, i * tile : i * tile + tile].astype(f32)
        mine_ref[rel, own, lanes] = again.astype(bf16)
        product = jnp.dot(gated[half(1 - core)], buffer[i], preferred_element_type=f32)
        other_ref[rel, :, lanes] = product.astype(bf16)


def attention(place, queries, key_rows, value_rows, out_gate, log_decay, attn_gain, out_weight, hidden_in, meta):
    heads = log_decay.shape[0]
    block = queries.shape[0]
    width = out_weight.shape[1]
    pieces = pl.pallas_call(
        state_kernel,
        out_shape=jax.ShapeDtypeStruct((2 * heads, 80, HD), bf16),
        compiler_params=pltpu.CompilerParams(vmem_limit_bytes=16 << 20),
    )(key_rows, value_rows, log_decay)
    pieces = lax.all_to_all(pieces, "seq", split_axis=0, concat_axis=0, tiled=True)
    before = pl.pallas_call(
        scan_kernel,
        out_shape=jax.ShapeDtypeStruct((2 * heads, 64, HD), bf16),
        compiler_params=pltpu.CompilerParams(vmem_limit_bytes=16 << 20),
    )(pieces)
    before = lax.all_to_all(before, "seq", split_axis=0, concat_axis=0, tiled=True)
    incoming = before.reshape(heads, HD, HD)
    tile = 768
    whole = lambda *shape: pl.BlockSpec(shape, lambda i, p: (0,) * len(shape))
    shapes = [(SIDE, 64, width // SIDE + 128), (SIDE, 64, width // SIDE)]
    return pieces, pl.pallas_call(
        mix_kernel,
        grid_spec=pltpu.PrefetchScalarGridSpec(
            num_scalar_prefetch=1,
            grid=(1,),
            in_specs=[whole(block, heads * HD)] * 4
            + [
                whole(heads, block),
                whole(heads, HD, HD),
                whole(1, heads * HD),
                whole(*hidden_in.shape),
                whole(*meta.shape),
                pl.BlockSpec(memory_space=pltpu.HBM),
            ],
            out_specs=[whole(*shape) for shape in shapes],
            scratch_shapes=[
                pltpu.VMEM((block, heads * HD), bf16),
                pltpu.VMEM((width // tile, heads * HD, tile), bf16),
                pltpu.SemaphoreType.DMA((width // tile,)),
            ],
        ),
        out_shape=[jax.ShapeDtypeStruct(shape, bf16) for shape in shapes],
        compiler_params=pltpu.CompilerParams(vmem_limit_bytes=26 << 20),
    )(
        place, queries, key_rows, value_rows, out_gate, log_decay, incoming, attn_gain.reshape(1, -1),
        hidden_in, meta, out_weight,
    )


def cut_kernel(layout, chips, *refs):
    sources, outs, sems = refs[: sum(layout)], refs[sum(layout) : -1], refs[-1]
    copies = []
    for i, (out, count) in enumerate(zip(outs, layout)):
        part = out.shape[2]
        lanes = pl.ds(pl.multiple_of(chips[i] * part, part), part)
        for j in range(count):
            copies.append(pltpu.make_async_copy(sources[j].at[:, lanes], out.at[j], sems.at[i, j]))
            copies[-1].start()
        sources = sources[count:]
    for copy in copies:
        copy.wait()


def cut(chips, wanted, part):
    units = wanted[0][0].shape[0]
    layout = [len(arrays) for arrays in wanted]
    shapes = [(count, units, part) for count in layout]
    outs = pl.pallas_call(
        functools.partial(cut_kernel, layout),
        grid_spec=pltpu.PrefetchScalarGridSpec(
            num_scalar_prefetch=1,
            grid=(1,),
            in_specs=[pl.BlockSpec(memory_space=pltpu.HBM)] * sum(layout),
            out_specs=[pl.BlockSpec(shape, lambda t, chips: (0, 0, 0)) for shape in shapes],
            scratch_shapes=[pltpu.SemaphoreType.DMA((len(layout), max(layout)))],
        ),
        out_shape=[jax.ShapeDtypeStruct(shape, bf16) for shape in shapes],
        compiler_params=pltpu.CompilerParams(vmem_limit_bytes=16 << 20),
    )(chips, *[array for arrays in wanted for array in arrays])
    return [out.reshape(-1, part) for out in outs]


def parts_of(refs, first, count):
    found, base, done = [], 0, 0
    for ref, begin, length in refs:
        low, high = max(first, base), min(first + count, base + length)
        if low < high:
            found.append((ref, begin + low - base, high - low, done))
            done += high - low
        base += length
    return found


def gate_up_kernel(layout, units, ids, *refs):
    x_count, holds, done = layout
    x_refs, refs = refs[:x_count], refs[x_count:]
    done_refs, refs = refs[:done], refs[done:]
    pieces = []
    for begins in holds:
        n = len(begins)
        pieces.append([(ref, begin, 2 * units // n) for ref, begin in zip(refs[:n], begins)])
        refs = refs[n:]
    out_ref, buffer, rows, acc, tails, sems, x_sems, done_sem = refs
    kept = 0
    for ref in done_refs:
        kept = ref.shape[1]
        done_copy = pltpu.make_async_copy(ref, out_ref.at[:, pl.ds(0, kept)], done_sem)
        done_copy.start()
    depth = buffer.shape[2]
    x_copies = []
    start = 0
    for i, ref in enumerate(x_refs):
        for j in range(ref.shape[0]):
            copy = pltpu.make_async_copy(ref.at[j], rows.at[pl.ds(start, 64)], x_sems.at[i, j])
            copy.start()
            x_copies.append(copy)
            start += 64
    wide = 2 * units
    edge = wide // 128 * 128
    rest = wide - edge
    copies = []
    for i, arrays in enumerate(pieces):
        pair, which = i // 2, i % 2
        moves = []
        for first, count, there in ((0, edge, which * edge), (edge, rest, 2 * edge + which * rest)):
            for ref, low, n, before in parts_of(arrays, first, count):
                moves.append((ref.at[pl.ds(low, n)], buffer.at[pair, pl.ds(there + before, n)]))
        copies.append([])
        for j, (source, target) in enumerate(moves):
            copy = pltpu.make_async_copy(source, target, sems.at[i, j])
            copy.start()
            copies[-1].append(copy)
    total = rows.shape[0]
    for copy in x_copies:
        copy.wait()
    tile = 256
    for pair in range(len(pieces) // 2):
        for which in range(2):
            for copy in copies[2 * pair + which]:
                copy.wait()
        experts = [ids[2 + 2 * pair + which].astype(f32) for which in range(2)]

        @pl.loop(0, total // tile)
        def _(t):
            at = pl.ds(pl.multiple_of(t * tile, tile), tile)
            part = dot_nt(rows[at, :depth], buffer[pair])
            meta = rows[at, depth:].astype(f32)
            last = part[:, 2 * edge :]
            turned = pltpu.roll(last, rest, 1)
            for k in range(2):
                named = [meta[:, 64 + k : 65 + k] == expert for expert in experts]
                acc[k, at] = jnp.where(
                    named[0], part[:, :edge], jnp.where(named[1], part[:, edge : 2 * edge], acc[k, at])
                )
                tails[k, at] = jnp.where(named[0], last, jnp.where(named[1], turned, tails[k, at]))

    @pl.loop(0, total // tile)
    def _(t):
        at = pl.ds(pl.multiple_of(t * tile, tile), tile)
        lane = lax.broadcasted_iota(jnp.int32, (tile, 128), 1)
        for k in range(2):
            last = jnp.where(lane < rest, tails[k, at], rows[at, depth:].astype(f32)).astype(bf16)
            head = acc[k, at].astype(bf16)
            lanes = k * (edge + 128)
            for i in range(SIDE):
                rel = lax.rem(i + SIDE - ids[0], SIDE)
                cut = slice(i * 64, i * 64 + 64)
                out_ref[rel, kept + t, :, lanes : lanes + edge] = head[cut]
                out_ref[rel, kept + t, :, lanes + edge : lanes + edge + 128] = last[cut]

    if kept:
        done_copy.wait()


def gate_up(ids, xs, pieces, units, done=()):
    blocks = sum(x.shape[0] for x in xs)
    depth = pieces[0][0][0].shape[1]
    edge = 2 * units // 128 * 128
    whole = lambda shape: pl.BlockSpec(shape, lambda i, p: (0,) * len(shape))
    kept = sum(y.shape[1] for y in done)
    shape = (SIDE, kept + blocks // SIDE, 64, 2 * (edge + 128))
    flat = [array for arrays in pieces for array, _ in arrays]
    return pl.pallas_call(
        functools.partial(gate_up_kernel, (len(xs), [[begin for _, begin in arrays] for arrays in pieces], len(done)), units),
        grid_spec=pltpu.PrefetchScalarGridSpec(
            num_scalar_prefetch=1,
            grid=(1,),
            in_specs=[pl.BlockSpec(memory_space=pl.ANY)] * (len(xs) + len(done))
            + [pl.BlockSpec(memory_space=pltpu.HBM)] * len(flat),
            out_specs=whole(shape),
            scratch_shapes=[
                pltpu.VMEM((len(pieces) // 2, 4 * units, depth), bf16),
                pltpu.VMEM((blocks * 64, xs[0].shape[2]), bf16),
                pltpu.VMEM((2, blocks * 64, edge), f32),
                pltpu.VMEM((2, blocks * 64, 128), f32),
                pltpu.SemaphoreType.DMA((len(pieces), 4)),
                pltpu.SemaphoreType.DMA((len(xs), SIDE)),
                pltpu.SemaphoreType.DMA,
            ],
        ),
        out_shape=jax.ShapeDtypeStruct(shape, bf16),
        cost_estimate=pl.CostEstimate(
            flops=2 * blocks * 64 * depth * units * 16, bytes_accessed=20 << 20, transcendentals=0
        ),
        compiler_params=pltpu.CompilerParams(vmem_limit_bytes=34 << 20),
    )(ids, *xs, *done, *flat)


def down_kernel(layout, units, ids, *refs):
    h_count, firsts = layout
    h_refs, pieces, (out_ref, buffer, spread, sems) = refs[:h_count], refs[h_count:-4], refs[-4:]
    pad = buffer.shape[1]
    copies = []
    for i, (ref, first) in enumerate(zip(pieces, firsts)):
        copy = pltpu.make_async_copy(ref.at[pl.ds(first, units)], buffer.at[i, pl.ds(0, units)], sems.at[i])
        copy.start()
        copies.append(copy)
    groups = h_refs[0].shape[0]
    rows = groups * 64
    for j, ref in enumerate(h_refs):
        h = ref[...].reshape(rows, ref.shape[2]).astype(f32)
        first = h[:, units : units + 1]
        second = h[:, units + 1 : units + 2]
        for i in range(8):
            expert = ids[2 + i].astype(f32)
            kept = jnp.where(first == expert, h[:, :pad], jnp.where(second == expert, h[:, pad:], 0.0))
            spread[j * rows : j * rows + rows, i * pad : i * pad + pad] = kept.astype(bf16)
    for i in range(8):
        buffer[i, units:, :] = jnp.zeros((pad - units, buffer.shape[2]), bf16)
    for copy in copies:
        copy.wait()
    weights = buffer.reshape(8 * pad, buffer.shape[2])
    tile = 512
    for n in range(buffer.shape[2] // tile):
        lanes = pl.ds(n * tile, tile)
        for j in range(h_count):
            part = spread[j * rows : j * rows + rows]
            result = jnp.dot(part, weights[:, lanes], preferred_element_type=f32).astype(bf16)
            for g in range(groups):
                out_ref[g, ids[10 + j], :, lanes] = result[g * 64 : g * 64 + 64]


def down(ids, hidden, pieces, firsts, units):
    width = pieces[0].shape[1]
    pad = units + -units % 128
    groups = hidden[0].shape[0]
    shape = (groups, SIDE, 64, width)
    whole = lambda shape: pl.BlockSpec(shape, lambda i, p: (0,) * len(shape))
    return pl.pallas_call(
        functools.partial(down_kernel, (len(hidden), firsts), units),
        grid_spec=pltpu.PrefetchScalarGridSpec(
            num_scalar_prefetch=1,
            grid=(1,),
            in_specs=[whole(h.shape) for h in hidden] + [pl.BlockSpec(memory_space=pltpu.HBM)] * 8,
            out_specs=whole(shape),
            scratch_shapes=[
                pltpu.VMEM((8, pad, width), bf16),
                pltpu.VMEM((groups * SIDE * 64, 8 * pad), bf16),
                pltpu.SemaphoreType.DMA((8,)),
            ],
        ),
        out_shape=jax.ShapeDtypeStruct(shape, bf16),
        cost_estimate=pl.CostEstimate(
            flops=2 * groups * 4 * 64 * 8 * pad * width, bytes_accessed=12 << 20, transcendentals=0
        ),
        compiler_params=pltpu.CompilerParams(vmem_limit_bytes=32 << 20),
    )(ids, *hidden, *pieces)


def fan(value, perm):
    far = send(value, perm(2))
    return send(value, perm(1)), send(value, perm(-1)), far


def plus(a, b):
    return (a.astype(f32) + b.astype(f32)).astype(bf16)


def deliver(behind, ahead, far, perm):
    far = send(far, perm(2))
    got = send(ahead, perm(1)), send(behind, perm(-1)), far
    return got[0].astype(f32) + got[1].astype(f32) + got[2].astype(f32)


def after(value, *others):
    return lax.optimization_barrier((value, others))[0]


def fetch_sum(own, behind, ahead, far, perm):
    far = send(far, perm(2))
    return [own, send(ahead, perm(1)), send(behind, perm(-1)), far]


def join_kernel(own, right, left, far, gain_ref, rows_ref, mid_ref):
    part = mid_ref.shape[1]
    total = own[...].astype(f32) + right[...].astype(f32) + left[...].astype(f32) + far[...].astype(f32)
    mid = total[:, :part].astype(bf16)
    mid_ref[...] = mid
    mid = mid.astype(f32)
    rows_ref[:, :part] = (mid * gain_ref[...]).astype(bf16)
    squares = jnp.sum(mid * mid, axis=1, keepdims=True)
    high = squares.astype(bf16).astype(f32)
    lane = lax.broadcasted_iota(jnp.int32, (rows_ref.shape[0], 128), 1)
    tail = jnp.where(lane == 72, high, jnp.where(lane == 73, squares - high, total[:, part:]))
    rows_ref[:, part:] = tail.astype(bf16)


def join(values, gain):
    count, width = values[0].shape
    return pl.pallas_call(
        join_kernel,
        out_shape=[jax.ShapeDtypeStruct((count, n), bf16) for n in (width, width - 128)],
        compiler_params=pltpu.CompilerParams(vmem_limit_bytes=8 << 20),
    )(*values, gain.reshape(1, -1))


def activate_kernel(units, width, own, right, left, far, out_ref):
    total = own[...].astype(f32) + right[...].astype(f32) + left[...].astype(f32) + far[...].astype(f32)
    total = total.reshape(-1, total.shape[2])
    col = total.shape[1] // 2
    wide = 2 * units
    pad = out_ref.shape[2] // 2
    scale = lax.rsqrt((total[:, wide + 8 : wide + 9] + total[:, wide + 9 : wide + 10]) / width + 1e-06)
    lane = lax.broadcasted_iota(jnp.int32, (total.shape[0], pad), 1)
    for k in range(2):
        both = total[:, k * col : k * col + col]
        gate = both[:, :pad] * scale
        up = pltpu.roll(both, col - units, 1)[:, :pad] * scale
        at = wide + 2 + 3 * k
        weight = total[:, at : at + 1] + total[:, at + 1 : at + 2] + total[:, at + 2 : at + 3]
        value = gate / (1.0 + jnp.exp(-gate)) * up * (weight * (1.0 / SIDE))
        for j in range(2):
            route = total[:, wide + j : wide + j + 1] * (1.0 / SIDE)
            value = jnp.where(lane == units + j, route, value)
        value = jnp.where(lane < units + 2, value, 0.0)
        out_ref[:, :, k * pad : k * pad + pad] = value.astype(bf16).reshape(out_ref.shape[:2] + (pad,))


def activate(values, units, width):
    pad = units + -units % 128
    return pl.pallas_call(
        functools.partial(activate_kernel, units, width),
        out_shape=jax.ShapeDtypeStruct(values[0].shape[:2] + (2 * pad,), bf16),
        compiler_params=pltpu.CompilerParams(vmem_limit_bytes=24 << 20),
    )(*values)


def per_device(
    hidden_in,
    queries,
    key_rows,
    value_rows,
    out_gate,
    log_decay,
    attn_gain,
    out_weight,
    ffn_gain,
    routes,
    combine_weight,
    gate_weight,
    up_weight,
    down_weight,
):
    width = hidden_in.shape[1]
    part = width // SIDE
    units = gate_weight.shape[2]
    at = lax.axis_index("exp")
    x, core = at // CORES, lax.rem(at, CORES)
    order = [0, -1, 1, 2]
    chips = [lax.rem(x + d + SIDE, SIDE) for d in order]
    place = jnp.stack(
        [x, core]
        + [e for chip in chips for e in (2 * chip + core, 2 * chip + 1 - core)]
        + chips
    ).astype(jnp.int32)

    gate_t, up_t, down_w = gate_weight[0].T, up_weight[0].T, down_weight[0]

    at_chip = lambda *ds: jnp.stack([lax.rem(x + d + SIDE, SIDE) for d in ds]).astype(jnp.int32)
    gate_up_t = [gate_t, up_t]

    to_ahead, to_behind, to_far = cut(at_chip(1, -1, 2), [gate_up_t, gate_up_t, [gate_t]], part)
    w_behind, w_ahead = send(to_ahead, along_x(1)), send(to_behind, along_x(-1))
    w_gate = send(to_far, along_x(2))

    toks = hidden_in.shape[0]
    routes_f = routes.astype(f32)
    cw = split3(combine_weight)
    lanes = [routes_f[:, 0:1], routes_f[:, 1:2]] + [w[:, k : k + 1] for k in range(2) for w in cw]
    meta = jnp.concatenate([jnp.zeros((toks, 64), f32)] + lanes + [jnp.zeros((toks, 64 - len(lanes)), f32)], 1)
    key_rows, to_ahead, to_behind, to_far = lax.optimization_barrier((key_rows, to_ahead, to_behind, to_far))
    _, (mine, other) = attention(
        place, queries, key_rows, value_rows, out_gate, log_decay, attn_gain, out_weight, hidden_in,
        meta.astype(bf16),
    )
    w_behind, w_ahead, w_gate, mine, other = lax.optimization_barrier((w_behind, w_ahead, w_gate, mine, other))
    other = send(other, OTHER_CORE)
    summed = jnp.concatenate([plus(mine[:, :, :part], other), mine[:, :, part:]], 2)
    (w_mine,) = cut(after(at_chip(0), summed), [gate_up_t + [down_w]], part)
    first = jnp.concatenate([w_behind, w_ahead, w_gate], 0)
    gain = lax.dynamic_slice(ffn_gain, (x * part,), (part,))
    values = fetch_sum(summed[0], summed[3], summed[1], summed[2], along_x)
    values, w_mine, first = lax.optimization_barrier((values, w_mine, first))
    rows, mid = join(values, gain)
    mid_f = mid.astype(f32)

    (to_far,) = cut(after(at_chip(2), mid), [[up_t]], part)
    w_up = send(to_far, along_x(2))
    s_first = send(first, OTHER_CORE)
    plane = jnp.stack([rows, *fan(rows, along_first)])
    w_up, s_first, plane = lax.optimization_barrier((w_up, s_first, plane))
    s_up = send(w_up, OTHER_CORE)
    s_mine = send(w_mine, OTHER_CORE)
    to_ahead, to_behind = cut(after(at_chip(1, -1), plane), [[down_w], [down_w]], part)
    d_behind, d_ahead = send(to_ahead, along_x(1)), send(to_behind, along_x(-1))
    right, left = send(plane, along_second(1)), send(plane, along_second(-1))
    wide = 2 * units
    weights = [((w_mine, 0),), ((s_mine, 0),), ((w_behind, 0),), ((s_first, 0),)]
    weights += [((w_ahead, 0),), ((s_first, wide),), ((w_gate, 0), (w_up, 0)), ((s_first, 2 * wide), (s_up, 0))]
    y_first = gate_up(place, [plane], weights, units)
    right, left = lax.optimization_barrier((right, left))
    far = send(right[:2], along_second(1)), send(left[2:], along_second(-1))
    d_behind, d_ahead, y_first = lax.optimization_barrier((d_behind, d_ahead, y_first))
    (to_far,) = cut(after(at_chip(2), y_first), [[down_w]], part)
    d_far = send(to_far, along_x(2))
    y = gate_up(place, [right, left], weights, units, [y_first])
    far, d_far, y = lax.optimization_barrier((far, d_far, y))

    def middle(y):
        return activate(fetch_sum(y[0], y[3], y[1], y[2], along_x), units, width)

    y_last = gate_up(place, far, weights, units)
    hidden = middle(y)
    hidden, y_last = lax.optimization_barrier((hidden, y_last))
    d_swaps = [send(d, OTHER_CORE) for d in (d_behind, d_ahead, d_far)]
    hidden = [hidden, *fan(hidden, along_x)]
    hidden_last = middle(y_last)
    hidden_last = [hidden_last, *fan(hidden_last, along_x)]
    down_pieces = [w_mine, s_mine, d_behind, d_swaps[0], d_ahead, d_swaps[1], d_far, d_swaps[2]]
    firsts = [2 * units] * 2 + [0] * 6
    out = down(place, hidden, down_pieces, firsts, units)
    got = send(out[2], along_second(1)).astype(f32) + send(out[1], along_second(-1)).astype(f32)
    last = down(place, hidden_last, down_pieces, firsts, units)
    out = out[0].astype(f32) + (got + send(last[0], along_second(2)).astype(f32))
    own = out[0]
    out = out.astype(bf16)
    out = own + deliver(out[1], out[2], out[3], along_first)
    out = (mid_f + out).astype(bf16).reshape(SIDE, toks, part)
    pick = lambda d: lax.dynamic_index_in_dim(out, chips[order.index(d)], 0, False)
    far = send(pick(2), along_x(2))
    columns = jnp.stack([pick(0), send(pick(-1), along_x(-1)), far, send(pick(1), along_x(1))])
    columns = jnp.roll(columns, x, axis=0)
    return columns.transpose(1, 0, 2).reshape(toks, width)


def solution(mesh):
    return jax.shard_map(
        per_device,
        mesh=mesh,
        in_specs=(
            P(("seq", "exp"), None),
            P("seq", "exp"),
            P("seq", "exp"),
            P("seq", "exp"),
            P("seq", "exp"),
            P("exp", "seq"),
            P("exp"),
            P("exp", None),
            P(),
            P(("seq", "exp"), None),
            P(("seq", "exp"), None),
            P("exp", None, "seq"),
            P("exp", None, "seq"),
            P("exp", "seq", None),
        ),
        out_specs=P(("seq", "exp"), None),
        check_vma=False,
    )
```

```python
import functools

import jax
import jax.numpy as jnp
from jax import lax
from jax.experimental import pallas as pl
from jax.experimental.pallas import tpu as pltpu
from jax.sharding import PartitionSpec as P

f32 = jnp.float32
bf16 = jnp.bfloat16
SIDE = 4
CORES = 2
AXES = ("seq", "exp")
HD = 128


def permutation(move):
    pairs = []
    for z in range(SIDE):
        for y in range(SIDE):
            for x in range(SIDE):
                for c in range(CORES):
                    z2, y2, x2, c2 = move(z, y, x, c)
                    source = ((z * SIDE + y) * SIDE + x) * CORES + c
                    target = (((z2 % SIDE) * SIDE + y2 % SIDE) * SIDE + x2 % SIDE) * CORES + c2
                    pairs.append((source, target))
    return pairs


def along_x(k):
    return permutation(lambda z, y, x, c: (z, y, x + k, c))


def along_first(k):
    return permutation(lambda z, y, x, c: (z, y + k, x, c) if c == 0 else (z + k, y, x, c))


def along_second(k):
    return permutation(lambda z, y, x, c: (z + k, y, x, c) if c == 0 else (z, y + k, x, c))


OTHER_CORE = permutation(lambda z, y, x, c: (z, y, x, 1 - c))


def send(value, perm):
    return lax.ppermute(value, AXES, perm)


def split3(value):
    high = lax.reduce_precision(value, 8, 7)
    rest = value - high
    mid = lax.reduce_precision(rest, 8, 7)
    return high, mid, rest - mid


def lower_triangle(n):
    row = lax.broadcasted_iota(jnp.int32, (n, n), 0)
    col = lax.broadcasted_iota(jnp.int32, (n, n), 1)
    return row >= col


def dot_nt(a, b, **kw):
    return lax.dot_general(a, b, (((1,), (1,)), ((), ())), preferred_element_type=f32, **kw)


def dot_tn(a, b, **kw):
    return lax.dot_general(a, b, (((0,), (0,)), ((), ())), preferred_element_type=f32, **kw)


def state_kernel(k_ref, v_ref, ld_ref, out_ref):
    heads, block = ld_ref.shape
    low = lower_triangle(block).astype(f32)
    ld = ld_ref[...]
    cum_col = dot_nt(low, ld, precision=lax.Precision.HIGHEST)
    ends = cum_col[block - 1 : block, :]
    factor = jnp.exp(ends - cum_col)
    rows = lax.broadcasted_iota(jnp.int32, (16, HD), 0)
    for h in range(heads):
        lanes = pl.ds(h * HD, HD)
        keyed = (k_ref[:, lanes].astype(f32) * factor[:, h : h + 1]).astype(bf16)
        state = dot_tn(keyed, v_ref[:, lanes]).astype(bf16)
        end = jnp.broadcast_to(ends[:, h : h + 1], (16, HD))
        high = end.astype(bf16).astype(f32)
        rest = end - high
        mid = rest.astype(bf16).astype(f32)
        tail = jnp.where(rows == 0, high, jnp.where(rows == 1, mid, jnp.where(rows == 2, rest - mid, 0.0)))
        tail = tail.astype(bf16)
        for part in range(2):
            out_ref[2 * h + part, 0:64, :] = state[part * 64 : part * 64 + 64]
            out_ref[2 * h + part, 64:80, :] = tail


def scan_kernel(in_ref, out_ref):
    count = in_ref.shape[0]
    carry = jnp.zeros((64, HD), f32)
    for i in range(count):
        out_ref[i] = carry.astype(bf16)
        if i + 1 < count:
            tail = in_ref[i, 64:80, :].astype(f32)
            end = tail[0:1] + tail[1:2] + tail[2:3]
            carry = jnp.exp(end) * carry + in_ref[i, 0:64, :].astype(f32)


def mix_kernel(
    place, q_ref, k_ref, v_ref, g_ref, ld_ref, inc_ref, gain_ref, hid_ref, meta_ref, w_ref,
    mine_ref, other_ref, gated, buffer, sems,
):
    heads, block = ld_ref.shape
    tiles = buffer.shape[0]
    tile = buffer.shape[2]
    copies = [
        pltpu.make_async_copy(w_ref.at[:, pl.ds(i * tile, tile)], buffer.at[i], sems.at[i]) for i in range(tiles)
    ]
    for copy in copies:
        copy.start()
    causal = lower_triangle(block)
    low = causal.astype(f32)
    ld = ld_ref[...]
    cum_col = dot_nt(low, ld, precision=lax.Precision.HIGHEST)
    cum_row = dot_nt(ld, low, precision=lax.Precision.HIGHEST)
    grown = jnp.exp(cum_col)
    for h in range(heads):
        lanes = pl.ds(h * HD, HD)
        q, k, v = q_ref[:, lanes], k_ref[:, lanes], v_ref[:, lanes]
        spread = cum_col[:, h : h + 1] - cum_row[h : h + 1, :]
        weights = jnp.where(causal, dot_nt(q, k) * jnp.exp(jnp.where(causal, spread, 0.0)), 0.0)
        intra = jnp.dot(weights.astype(bf16), v, preferred_element_type=f32)
        inter = jnp.dot(q, inc_ref[h], preferred_element_type=f32) * grown[:, h : h + 1]
        mixed = intra + inter
        normal = mixed * lax.rsqrt(jnp.mean(mixed * mixed, axis=-1, keepdims=True) + 1e-05)
        gate = 1.0 / (1.0 + jnp.exp(-g_ref[:, lanes].astype(f32)))
        result = (normal * gain_ref[:, lanes] * gate).astype(bf16)
        for x in range(SIDE):
            for c in range(CORES):
                there = pl.multiple_of(lax.rem(c + place[1], CORES) * 64 + x * 16, 16)
                gated[pl.ds(there, 16), lanes] = result[x * 32 + c * 16 : x * 32 + c * 16 + 16]
    toks = hid_ref.shape[0]
    own = pl.ds(pl.multiple_of(place[0] * toks, toks), toks)
    per = tiles // SIDE
    width = per * tile
    for rel in range(SIDE):
        mine_ref[rel, :, width:] = jnp.zeros((64, 128), bf16)
        mine_ref[rel, own, width:] = meta_ref[...]
    for i in range(tiles):
        copies[i].wait()
        rel = lax.rem(i // per + SIDE - place[0], SIDE)
        lanes = pl.ds(i % per * tile, tile)
        product = jnp.dot(gated[...], buffer[i], preferred_element_type=f32)
        mine_ref[rel, :, lanes] = product[:64].astype(bf16)
        again = mine_ref[rel, own, lanes].astype(f32) + hid_ref[:, i * tile : i * tile + tile].astype(f32)
        mine_ref[rel, own, lanes] = again.astype(bf16)
        other_ref[rel, :, lanes] = product[64:].astype(bf16)


def block_states(key_rows, value_rows, log_decay):
    heads = log_decay.shape[0]
    pieces = pl.pallas_call(
        state_kernel,
        out_shape=jax.ShapeDtypeStruct((2 * heads, 80, HD), bf16),
        compiler_params=pltpu.CompilerParams(vmem_limit_bytes=16 << 20),
    )(key_rows, value_rows, log_decay)
    return lax.all_to_all(pieces, "seq", split_axis=0, concat_axis=0, tiled=True)


def earlier_states(pieces):
    before = pl.pallas_call(
        scan_kernel,
        out_shape=jax.ShapeDtypeStruct((pieces.shape[0], 64, HD), bf16),
        compiler_params=pltpu.CompilerParams(vmem_limit_bytes=16 << 20),
    )(pieces)
    before = lax.all_to_all(before, "seq", split_axis=0, concat_axis=0, tiled=True)
    return before.reshape(-1, HD, HD)


def attention(
    place, incoming, queries, key_rows, value_rows, out_gate, log_decay, attn_gain, out_weight, hidden_in, meta
):
    heads = log_decay.shape[0]
    block = queries.shape[0]
    width = out_weight.shape[1]
    tile = 768
    whole = lambda *shape: pl.BlockSpec(shape, lambda i, p: (0,) * len(shape))
    shapes = [(SIDE, 64, width // SIDE + 128), (SIDE, 64, width // SIDE)]
    return pl.pallas_call(
        mix_kernel,
        grid_spec=pltpu.PrefetchScalarGridSpec(
            num_scalar_prefetch=1,
            grid=(1,),
            in_specs=[whole(block, heads * HD)] * 4
            + [
                whole(heads, block),
                whole(heads, HD, HD),
                whole(1, heads * HD),
                whole(*hidden_in.shape),
                whole(*meta.shape),
                pl.BlockSpec(memory_space=pltpu.HBM),
            ],
            out_specs=[whole(*shape) for shape in shapes],
            scratch_shapes=[
                pltpu.VMEM((block, heads * HD), bf16),
                pltpu.VMEM((width // tile, heads * HD, tile), bf16),
                pltpu.SemaphoreType.DMA((width // tile,)),
            ],
        ),
        out_shape=[jax.ShapeDtypeStruct(shape, bf16) for shape in shapes],
        compiler_params=pltpu.CompilerParams(vmem_limit_bytes=60 << 20),
    )(
        place, queries, key_rows, value_rows, out_gate, log_decay, incoming, attn_gain.reshape(1, -1),
        hidden_in, meta, out_weight,
    )


def cut_kernel(layout, chips, *refs):
    sources, outs, sems = refs[: sum(layout)], refs[sum(layout) : -1], refs[-1]
    copies = []
    for i, (out, count) in enumerate(zip(outs, layout)):
        part = out.shape[2]
        lanes = pl.ds(pl.multiple_of(chips[i] * part, part), part)
        for j in range(count):
            copies.append(pltpu.make_async_copy(sources[j].at[:, lanes], out.at[j], sems.at[i, j]))
            copies[-1].start()
        sources = sources[count:]
    for copy in copies:
        copy.wait()


def cut(chips, wanted, part):
    units = wanted[0][0].shape[0]
    layout = [len(arrays) for arrays in wanted]
    shapes = [(count, units, part) for count in layout]
    outs = pl.pallas_call(
        functools.partial(cut_kernel, layout),
        grid_spec=pltpu.PrefetchScalarGridSpec(
            num_scalar_prefetch=1,
            grid=(1,),
            in_specs=[pl.BlockSpec(memory_space=pltpu.HBM)] * sum(layout),
            out_specs=[pl.BlockSpec(shape, lambda t, chips: (0, 0, 0)) for shape in shapes],
            scratch_shapes=[pltpu.SemaphoreType.DMA((len(layout), max(layout)))],
        ),
        out_shape=[jax.ShapeDtypeStruct(shape, bf16) for shape in shapes],
        compiler_params=pltpu.CompilerParams(vmem_limit_bytes=60 << 20),
    )(chips, *[array for arrays in wanted for array in arrays])
    return [out.reshape(-1, part) for out in outs]


def parts_of(refs, first, count):
    found, base, done = [], 0, 0
    for ref, begin, length in refs:
        low, high = max(first, base), min(first + count, base + length)
        if low < high:
            found.append((ref, begin + low - base, high - low, done))
            done += high - low
        base += length
    return found


def gate_up_kernel(layout, units, ids, *refs):
    x_count, holds, done = layout
    x_refs, refs = refs[:x_count], refs[x_count:]
    done_refs, refs = refs[:done], refs[done:]
    pieces = []
    for begins in holds:
        n = len(begins)
        pieces.append([(ref, begin, 2 * units // n) for ref, begin in zip(refs[:n], begins)])
        refs = refs[n:]
    out_ref, buffer, rows, acc, tails, sems, x_sems, done_sem = refs
    kept = 0
    for ref in done_refs:
        kept = ref.shape[1]
        done_copy = pltpu.make_async_copy(ref, out_ref.at[:, pl.ds(0, kept)], done_sem)
        done_copy.start()
    depth = buffer.shape[2]
    x_copies = []
    start = 0
    for i, ref in enumerate(x_refs):
        for j in range(ref.shape[0]):
            copy = pltpu.make_async_copy(ref.at[j], rows.at[pl.ds(start, 64)], x_sems.at[i, j])
            copy.start()
            x_copies.append(copy)
            start += 64
    wide = 2 * units
    edge = wide // 128 * 128
    rest = wide - edge
    copies = []
    for i, arrays in enumerate(pieces):
        pair, which = i // 2, i % 2
        moves = []
        for first, count, there in ((0, edge, which * edge), (edge, rest, 2 * edge + which * rest)):
            for ref, low, n, before in parts_of(arrays, first, count):
                moves.append((ref.at[pl.ds(low, n)], buffer.at[pair, pl.ds(there + before, n)]))
        copies.append([])
        for j, (source, target) in enumerate(moves):
            copy = pltpu.make_async_copy(source, target, sems.at[i, j])
            copy.start()
            copies[-1].append(copy)
    total = rows.shape[0]
    for copy in x_copies:
        copy.wait()
    tile = 256
    for pair in range(len(pieces) // 2):
        for which in range(2):
            for copy in copies[2 * pair + which]:
                copy.wait()
        experts = [ids[2 + 2 * pair + which].astype(f32) for which in range(2)]

        @pl.loop(0, total // tile)
        def _(t):
            at = pl.ds(pl.multiple_of(t * tile, tile), tile)
            part = dot_nt(rows[at, :depth], buffer[pair])
            meta = rows[at, depth:].astype(f32)
            last = part[:, 2 * edge :]
            turned = pltpu.roll(last, rest, 1)
            for k in range(2):
                named = [meta[:, 64 + k : 65 + k] == expert for expert in experts]
                acc[k, at] = jnp.where(
                    named[0], part[:, :edge], jnp.where(named[1], part[:, edge : 2 * edge], acc[k, at])
                )
                tails[k, at] = jnp.where(named[0], last, jnp.where(named[1], turned, tails[k, at]))

    @pl.loop(0, total // tile)
    def _(t):
        at = pl.ds(pl.multiple_of(t * tile, tile), tile)
        lane = lax.broadcasted_iota(jnp.int32, (tile, 128), 1)
        for k in range(2):
            last = jnp.where(lane < rest, tails[k, at], rows[at, depth:].astype(f32)).astype(bf16)
            head = acc[k, at].astype(bf16)
            lanes = k * (edge + 128)
            for i in range(SIDE):
                rel = lax.rem(i + SIDE - ids[0], SIDE)
                cut = slice(i * 64, i * 64 + 64)
                out_ref[rel, kept + t, :, lanes : lanes + edge] = head[cut]
                out_ref[rel, kept + t, :, lanes + edge : lanes + edge + 128] = last[cut]

    if kept:
        done_copy.wait()


def gate_up(ids, xs, pieces, units, done=()):
    blocks = sum(x.shape[0] for x in xs)
    depth = pieces[0][0][0].shape[1]
    edge = 2 * units // 128 * 128
    whole = lambda shape: pl.BlockSpec(shape, lambda i, p: (0,) * len(shape))
    kept = sum(y.shape[1] for y in done)
    shape = (SIDE, kept + blocks // SIDE, 64, 2 * (edge + 128))
    flat = [array for arrays in pieces for array, _ in arrays]
    return pl.pallas_call(
        functools.partial(gate_up_kernel, (len(xs), [[begin for _, begin in arrays] for arrays in pieces], len(done)), units),
        grid_spec=pltpu.PrefetchScalarGridSpec(
            num_scalar_prefetch=1,
            grid=(1,),
            in_specs=[pl.BlockSpec(memory_space=pl.ANY)] * (len(xs) + len(done))
            + [pl.BlockSpec(memory_space=pltpu.HBM)] * len(flat),
            out_specs=whole(shape),
            scratch_shapes=[
                pltpu.VMEM((len(pieces) // 2, 4 * units, depth), bf16),
                pltpu.VMEM((blocks * 64, xs[0].shape[2]), bf16),
                pltpu.VMEM((2, blocks * 64, edge), f32),
                pltpu.VMEM((2, blocks * 64, 128), f32),
                pltpu.SemaphoreType.DMA((len(pieces), 4)),
                pltpu.SemaphoreType.DMA((len(xs), SIDE)),
                pltpu.SemaphoreType.DMA,
            ],
        ),
        out_shape=jax.ShapeDtypeStruct(shape, bf16),
        cost_estimate=pl.CostEstimate(
            flops=2 * blocks * 64 * depth * units * 16, bytes_accessed=20 << 20, transcendentals=0
        ),
        compiler_params=pltpu.CompilerParams(vmem_limit_bytes=34 << 20),
    )(ids, *xs, *done, *flat)


def down_kernel(layout, units, ids, *refs):
    h_count, firsts = layout
    h_refs, pieces, (out_ref, buffer, spread, sems) = refs[:h_count], refs[h_count:-4], refs[-4:]
    pad = buffer.shape[1]
    copies = []
    tile = 512
    for n in range(buffer.shape[2] // tile):
        lanes = pl.ds(n * tile, tile)
        copies.append([])
        for i, (ref, first) in enumerate(zip(pieces, firsts)):
            copy = pltpu.make_async_copy(
                ref.at[pl.ds(first, units), lanes], buffer.at[i, pl.ds(0, units), lanes], sems.at[n, i]
            )
            copy.start()
            copies[-1].append(copy)
    groups = h_refs[0].shape[0]
    rows = groups * 64
    for j, ref in enumerate(h_refs):
        h = ref[...].reshape(rows, ref.shape[2]).astype(f32)
        first = h[:, 2 * units : 2 * units + 1]
        second = h[:, 2 * units + 1 : 2 * units + 2]
        turned = pltpu.roll(h, h.shape[1] - units, 1)[:, :pad]
        for i in range(8):
            expert = ids[2 + i].astype(f32)
            kept = jnp.where(first == expert, h[:, :pad], jnp.where(second == expert, turned, 0.0))
            spread[j * rows : j * rows + rows, i * pad : i * pad + pad] = kept.astype(bf16)
    for i in range(8):
        buffer[i, units:, :] = jnp.zeros((pad - units, buffer.shape[2]), bf16)
    weights = buffer.reshape(8 * pad, buffer.shape[2])
    for n in range(buffer.shape[2] // tile):
        lanes = pl.ds(n * tile, tile)
        for copy in copies[n]:
            copy.wait()
        result = jnp.dot(spread[...], weights[:, lanes], preferred_element_type=f32).astype(bf16)
        for j in range(h_count):
            for g in range(groups):
                first = j * rows + g * 64
                out_ref[g, ids[10 + j], :, lanes] = result[first : first + 64]


def down(ids, hidden, pieces, firsts, units):
    width = pieces[0].shape[1]
    pad = units + -units % 128
    groups = hidden[0].shape[0]
    shape = (groups, SIDE, 64, width)
    whole = lambda shape: pl.BlockSpec(shape, lambda i, p: (0,) * len(shape))
    return pl.pallas_call(
        functools.partial(down_kernel, (len(hidden), firsts), units),
        grid_spec=pltpu.PrefetchScalarGridSpec(
            num_scalar_prefetch=1,
            grid=(1,),
            in_specs=[whole(h.shape) for h in hidden] + [pl.BlockSpec(memory_space=pltpu.HBM)] * 8,
            out_specs=whole(shape),
            scratch_shapes=[
                pltpu.VMEM((8, pad, width), bf16),
                pltpu.VMEM((groups * SIDE * 64, 8 * pad), bf16),
                pltpu.SemaphoreType.DMA((width // 512, 8)),
            ],
        ),
        out_shape=jax.ShapeDtypeStruct(shape, bf16),
        cost_estimate=pl.CostEstimate(
            flops=2 * groups * 4 * 64 * 8 * pad * width, bytes_accessed=12 << 20, transcendentals=0
        ),
        compiler_params=pltpu.CompilerParams(vmem_limit_bytes=32 << 20),
    )(ids, *hidden, *pieces)


def fan(value, perm):
    far = send(value, perm(2))
    return send(value, perm(1)), send(value, perm(-1)), far


def plus(a, b):
    return (a.astype(f32) + b.astype(f32)).astype(bf16)


def deliver(behind, ahead, far, perm):
    far = send(far, perm(2))
    got = send(ahead, perm(1)), send(behind, perm(-1)), far
    return got[0].astype(f32) + got[1].astype(f32) + got[2].astype(f32)


def after(value, *others):
    return lax.optimization_barrier((value, others))[0]


def fetch_sum(own, behind, ahead, far, perm):
    far = send(far, perm(2))
    return [own, send(ahead, perm(1)), send(behind, perm(-1)), far]


def join_kernel(own, right, left, far, gain_ref, rows_ref, mid_ref):
    part = mid_ref.shape[1]
    total = own[...].astype(f32) + right[...].astype(f32) + left[...].astype(f32) + far[...].astype(f32)
    mid = total[:, :part].astype(bf16)
    mid_ref[...] = mid
    mid = mid.astype(f32)
    rows_ref[:, :part] = (mid * gain_ref[...]).astype(bf16)
    squares = jnp.sum(mid * mid, axis=1, keepdims=True)
    high = squares.astype(bf16).astype(f32)
    lane = lax.broadcasted_iota(jnp.int32, (rows_ref.shape[0], 128), 1)
    tail = jnp.where(lane == 72, high, jnp.where(lane == 73, squares - high, total[:, part:]))
    rows_ref[:, part:] = tail.astype(bf16)


def join(values, gain):
    count, width = values[0].shape
    return pl.pallas_call(
        join_kernel,
        out_shape=[jax.ShapeDtypeStruct((count, n), bf16) for n in (width, width - 128)],
        compiler_params=pltpu.CompilerParams(vmem_limit_bytes=8 << 20),
    )(*values, gain.reshape(1, -1))


def activate_kernel(units, width, own, right, left, far, out_ref):
    total = own[...].astype(f32) + right[...].astype(f32) + left[...].astype(f32) + far[...].astype(f32)
    total = total.reshape(-1, total.shape[2])
    col = total.shape[1] // 2
    wide = 2 * units
    scale = lax.rsqrt((total[:, wide + 8 : wide + 9] + total[:, wide + 9 : wide + 10]) / width + 1e-06)
    lane = lax.broadcasted_iota(jnp.int32, (total.shape[0], col), 1)
    result = []
    for k in range(2):
        gate = total[:, k * col : k * col + col] * scale
        up = pltpu.roll(gate, col - units, 1)
        at = wide + 2 + 3 * k
        weight = total[:, at : at + 1] + total[:, at + 1 : at + 2] + total[:, at + 2 : at + 3]
        result.append(gate / (1.0 + jnp.exp(-gate)) * up * (weight * (1.0 / SIDE)))
    value = jnp.where(lane < units, result[0], pltpu.roll(result[1], units, 1))
    value = jnp.where(lane < wide, value, 0.0)
    for j in range(2):
        route = total[:, wide + j : wide + j + 1] * (1.0 / SIDE)
        value = jnp.where(lane == wide + j, route, value)
    out_ref[...] = value.astype(bf16).reshape(out_ref.shape)


def activate(values, units, width):
    return pl.pallas_call(
        functools.partial(activate_kernel, units, width),
        out_shape=jax.ShapeDtypeStruct(values[0].shape[:2] + (values[0].shape[2] // 2,), bf16),
        compiler_params=pltpu.CompilerParams(vmem_limit_bytes=24 << 20),
    )(*values)


def per_device(
    hidden_in,
    queries,
    key_rows,
    value_rows,
    out_gate,
    log_decay,
    attn_gain,
    out_weight,
    ffn_gain,
    routes,
    combine_weight,
    gate_weight,
    up_weight,
    down_weight,
):
    width = hidden_in.shape[1]
    part = width // SIDE
    units = gate_weight.shape[2]
    at = lax.axis_index("exp")
    x, core = at // CORES, lax.rem(at, CORES)
    order = [0, -1, 1, 2]
    chips = [lax.rem(x + d + SIDE, SIDE) for d in order]
    place = jnp.stack(
        [x, core]
        + [e for chip in chips for e in (2 * chip + core, 2 * chip + 1 - core)]
        + chips
    ).astype(jnp.int32)

    gate_t, up_t, down_w = gate_weight[0].T, up_weight[0].T, down_weight[0]

    at_chip = lambda *ds: jnp.stack([lax.rem(x + d + SIDE, SIDE) for d in ds]).astype(jnp.int32)
    gate_up_t = [gate_t, up_t]

    to_ahead, to_behind = cut(at_chip(1, -1), [[gate_t], [gate_t]], part)
    key_rows, to_ahead, to_behind = lax.optimization_barrier((key_rows, to_ahead, to_behind))
    g_behind, g_ahead = send(to_ahead, along_x(1)), send(to_behind, along_x(-1))

    toks = hidden_in.shape[0]
    routes_f = routes.astype(f32)
    cw = split3(combine_weight)
    lanes = [routes_f[:, 0:1], routes_f[:, 1:2]] + [w[:, k : k + 1] for k in range(2) for w in cw]
    meta = jnp.concatenate([jnp.zeros((toks, 64), f32)] + lanes + [jnp.zeros((toks, 64 - len(lanes)), f32)], 1)
    states = block_states(key_rows, value_rows, log_decay)
    up_ahead, up_behind, far_gate, w_mine, far_up, far_down, down_ahead, down_behind = cut(
        at_chip(1, -1, 2, 0, 2, 2, 1, -1),
        [[up_t], [up_t], [gate_t], gate_up_t + [down_w], [up_t], [down_w], [down_w], [down_w]],
        part,
    )
    states, g_behind, g_ahead, up_ahead, up_behind, far_gate, w_mine = lax.optimization_barrier(
        (states, g_behind, g_ahead, up_ahead, up_behind, far_gate, w_mine)
    )
    u_behind, u_ahead = send(up_ahead, along_x(1)), send(up_behind, along_x(-1))
    g_far = send(far_gate, along_x(2))
    s_mine = send(w_mine, OTHER_CORE)
    incoming = earlier_states(states)
    mine, other = attention(
        place, incoming, queries, key_rows, value_rows, out_gate, log_decay, attn_gain, out_weight, hidden_in,
        meta.astype(bf16),
    )
    u_behind, u_ahead, g_far, s_mine, mine, other = lax.optimization_barrier(
        (u_behind, u_ahead, g_far, s_mine, mine, other)
    )
    other = send(other, OTHER_CORE)
    summed = jnp.concatenate([plus(mine[:, :, :part], other), mine[:, :, part:]], 2)
    first = jnp.concatenate([g_behind, u_behind, g_ahead, u_ahead, g_far], 0)
    gain = lax.dynamic_slice(ffn_gain, (x * part,), (part,))
    values = fetch_sum(summed[0], summed[3], summed[1], summed[2], along_x)
    values, first, gain, far_up = lax.optimization_barrier((values, first, gain, far_up))
    rows, mid = join(values, gain)
    mid_f = mid.astype(f32)

    w_up = send(far_up, along_x(2))
    s_first = send(first, OTHER_CORE)
    plane = jnp.stack([rows, *fan(rows, along_first)])
    s_first, plane = lax.optimization_barrier((s_first, plane))
    right, left = send(plane, along_second(1)), send(plane, along_second(-1))
    w_up, right, left, down_ahead, down_behind, far_down = lax.optimization_barrier(
        (w_up, right, left, down_ahead, down_behind, far_down)
    )
    s_up = send(w_up, OTHER_CORE)
    far = send(right[:2], along_second(1)), send(left[2:], along_second(-1))
    d_behind, d_ahead = send(down_ahead, along_x(1)), send(down_behind, along_x(-1))
    d_far = send(far_down, along_x(2))
    wide = 2 * units
    weights = [((w_mine, 0),), ((s_mine, 0),), ((g_behind, 0), (u_behind, 0)), ((s_first, 0),)]
    weights += [((g_ahead, 0), (u_ahead, 0)), ((s_first, wide),), ((g_far, 0), (w_up, 0))]
    weights += [((s_first, 2 * wide), (s_up, 0))]
    y = gate_up(place, [plane, right, left], weights, units)
    far, y = lax.optimization_barrier((far, y))
    y_last = gate_up(place, far, weights, units)
    values = fetch_sum(y[0], y[3], y[1], y[2], along_x)
    values, d_behind, d_ahead, d_far, y_last = lax.optimization_barrier(
        (values, d_behind, d_ahead, d_far, y_last)
    )
    s_down = send(jnp.concatenate([d_behind, d_ahead, d_far], 0), OTHER_CORE)
    hidden = activate(values, units, width)
    hidden = [hidden, *fan(hidden, along_x)]
    values = fetch_sum(y_last[0], y_last[3], y_last[1], y_last[2], along_x)
    hidden, s_down, values = lax.optimization_barrier((hidden, s_down, values))
    hidden_last = activate(values, units, width)
    hidden_last = [hidden_last, *fan(hidden_last, along_x)]
    down_pieces = [w_mine, s_mine, d_behind, s_down, d_ahead, s_down, d_far, s_down]
    firsts = [wide, wide, 0, 0, 0, units, 0, wide]
    out = down(place, hidden, down_pieces, firsts, units)
    got = send(out[2], along_second(1)).astype(f32) + send(out[1], along_second(-1)).astype(f32)
    last = down(place, hidden_last, down_pieces, firsts, units)
    out = out[0].astype(f32) + (got + send(last[0], along_second(2)).astype(f32))
    own = out[0]
    out = out.astype(bf16)
    out = own + deliver(out[1], out[2], out[3], along_first)
    out = (mid_f + out).astype(bf16).reshape(SIDE, toks, part)
    pick = lambda d: lax.dynamic_index_in_dim(out, chips[order.index(d)], 0, False)
    far = send(pick(2), along_x(2))
    columns = jnp.stack([pick(0), send(pick(-1), along_x(-1)), far, send(pick(1), along_x(1))])
    columns = jnp.roll(columns, x, axis=0)
    return columns.transpose(1, 0, 2).reshape(toks, width)


def solution(mesh):
    return jax.shard_map(
        per_device,
        mesh=mesh,
        in_specs=(
            P(("seq", "exp"), None),
            P("seq", "exp"),
            P("seq", "exp"),
            P("seq", "exp"),
            P("seq", "exp"),
            P("exp", "seq"),
            P("exp"),
            P("exp", None),
            P(),
            P(("seq", "exp"), None),
            P(("seq", "exp"), None),
            P("exp", None, "seq"),
            P("exp", None, "seq"),
            P("exp", "seq", None),
        ),
        out_specs=P(("seq", "exp"), None),
        check_vma=False,
    )
```

```python
import functools

import jax
import jax.numpy as jnp
from jax import lax
from jax.experimental import pallas as pl
from jax.experimental.pallas import tpu as pltpu
from jax.sharding import PartitionSpec as P

f32 = jnp.float32
bf16 = jnp.bfloat16
SIDE = 4
CORES = 2
AXES = ("seq", "exp")
HD = 128


def permutation(move):
    pairs = []
    for z in range(SIDE):
        for y in range(SIDE):
            for x in range(SIDE):
                for c in range(CORES):
                    z2, y2, x2, c2 = move(z, y, x, c)
                    source = ((z * SIDE + y) * SIDE + x) * CORES + c
                    target = (((z2 % SIDE) * SIDE + y2 % SIDE) * SIDE + x2 % SIDE) * CORES + c2
                    pairs.append((source, target))
    return pairs


def along_x(k):
    return permutation(lambda z, y, x, c: (z, y, x + k, c))


def along_first(k):
    return permutation(lambda z, y, x, c: (z, y + k, x, c) if c == 0 else (z + k, y, x, c))


def along_second(k):
    return permutation(lambda z, y, x, c: (z + k, y, x, c) if c == 0 else (z, y + k, x, c))


OTHER_CORE = permutation(lambda z, y, x, c: (z, y, x, 1 - c))


def send(value, perm):
    return lax.ppermute(value, AXES, perm)


def split3(value):
    high = lax.reduce_precision(value, 8, 7)
    rest = value - high
    mid = lax.reduce_precision(rest, 8, 7)
    return high, mid, rest - mid


def lower_triangle(n):
    row = lax.broadcasted_iota(jnp.int32, (n, n), 0)
    col = lax.broadcasted_iota(jnp.int32, (n, n), 1)
    return row >= col


def dot_nt(a, b, **kw):
    return lax.dot_general(a, b, (((1,), (1,)), ((), ())), preferred_element_type=f32, **kw)


def dot_tn(a, b, **kw):
    return lax.dot_general(a, b, (((0,), (0,)), ((), ())), preferred_element_type=f32, **kw)


def state_kernel(k_ref, v_ref, ld_ref, out_ref):
    heads, block = ld_ref.shape
    low = lower_triangle(block).astype(f32)
    ld = ld_ref[...]
    cum_col = dot_nt(low, ld, precision=lax.Precision.HIGHEST)
    ends = cum_col[block - 1 : block, :]
    factor = jnp.exp(ends - cum_col)
    rows = lax.broadcasted_iota(jnp.int32, (16, HD), 0)
    for h in range(heads):
        lanes = pl.ds(h * HD, HD)
        keyed = (k_ref[:, lanes].astype(f32) * factor[:, h : h + 1]).astype(bf16)
        state = dot_tn(keyed, v_ref[:, lanes]).astype(bf16)
        end = jnp.broadcast_to(ends[:, h : h + 1], (16, HD))
        high = end.astype(bf16).astype(f32)
        rest = end - high
        mid = rest.astype(bf16).astype(f32)
        tail = jnp.where(rows == 0, high, jnp.where(rows == 1, mid, jnp.where(rows == 2, rest - mid, 0.0)))
        tail = tail.astype(bf16)
        for part in range(2):
            out_ref[2 * h + part, 0:64, :] = state[part * 64 : part * 64 + 64]
            out_ref[2 * h + part, 64:80, :] = tail


def scan_kernel(in_ref, out_ref):
    count = in_ref.shape[0]
    carry = jnp.zeros((64, HD), f32)
    for i in range(count):
        out_ref[i] = carry.astype(bf16)
        if i + 1 < count:
            tail = in_ref[i, 64:80, :].astype(f32)
            end = tail[0:1] + tail[1:2] + tail[2:3]
            carry = jnp.exp(end) * carry + in_ref[i, 0:64, :].astype(f32)


def mix_kernel(
    place, q_ref, k_ref, v_ref, g_ref, ld_ref, inc_ref, gain_ref, hid_ref, meta_ref, w_ref,
    mine_ref, other_ref, gated, buffer, sems,
):
    heads, block = ld_ref.shape
    tiles = buffer.shape[0]
    tile = buffer.shape[2]
    copies = [
        pltpu.make_async_copy(w_ref.at[:, pl.ds(i * tile, tile)], buffer.at[i], sems.at[i]) for i in range(tiles)
    ]
    for copy in copies:
        copy.start()
    causal = lower_triangle(block)
    low = causal.astype(f32)
    ld = ld_ref[...]
    cum_col = dot_nt(low, ld, precision=lax.Precision.HIGHEST)
    cum_row = dot_nt(ld, low, precision=lax.Precision.HIGHEST)
    grown = jnp.exp(cum_col)
    for h in range(heads):
        lanes = pl.ds(h * HD, HD)
        q, k, v = q_ref[:, lanes], k_ref[:, lanes], v_ref[:, lanes]
        spread = cum_col[:, h : h + 1] - cum_row[h : h + 1, :]
        weights = jnp.where(causal, dot_nt(q, k) * jnp.exp(jnp.where(causal, spread, 0.0)), 0.0)
        intra = jnp.dot(weights.astype(bf16), v, preferred_element_type=f32)
        inter = jnp.dot(q, inc_ref[h], preferred_element_type=f32) * grown[:, h : h + 1]
        mixed = intra + inter
        normal = mixed * lax.rsqrt(jnp.mean(mixed * mixed, axis=-1, keepdims=True) + 1e-05)
        gate = 1.0 / (1.0 + jnp.exp(-g_ref[:, lanes].astype(f32)))
        result = (normal * gain_ref[:, lanes] * gate).astype(bf16)
        for x in range(SIDE):
            for c in range(CORES):
                there = pl.multiple_of(lax.rem(c + place[1], CORES) * 64 + x * 16, 16)
                gated[pl.ds(there, 16), lanes] = result[x * 32 + c * 16 : x * 32 + c * 16 + 16]
    toks = hid_ref.shape[0]
    own = pl.ds(pl.multiple_of(place[0] * toks, toks), toks)
    per = tiles // SIDE
    width = per * tile
    for rel in range(SIDE):
        mine_ref[rel, :, width:] = jnp.zeros((64, 128), bf16)
        mine_ref[rel, own, width:] = meta_ref[...]
    for i in range(tiles):
        copies[i].wait()
        rel = lax.rem(i // per + SIDE - place[0], SIDE)
        lanes = pl.ds(i % per * tile, tile)
        product = jnp.dot(gated[...], buffer[i], preferred_element_type=f32)
        mine_ref[rel, :, lanes] = product[:64].astype(bf16)
        again = mine_ref[rel, own, lanes].astype(f32) + hid_ref[:, i * tile : i * tile + tile].astype(f32)
        mine_ref[rel, own, lanes] = again.astype(bf16)
        other_ref[rel, :, lanes] = product[64:].astype(bf16)


def block_states(key_rows, value_rows, log_decay):
    heads = log_decay.shape[0]
    pieces = pl.pallas_call(
        state_kernel,
        out_shape=jax.ShapeDtypeStruct((2 * heads, 80, HD), bf16),
        compiler_params=pltpu.CompilerParams(vmem_limit_bytes=16 << 20),
    )(key_rows, value_rows, log_decay)
    return lax.all_to_all(pieces, "seq", split_axis=0, concat_axis=0, tiled=True)


def earlier_states(pieces):
    before = pl.pallas_call(
        scan_kernel,
        out_shape=jax.ShapeDtypeStruct((pieces.shape[0], 64, HD), bf16),
        compiler_params=pltpu.CompilerParams(vmem_limit_bytes=16 << 20),
    )(pieces)
    before = lax.all_to_all(before, "seq", split_axis=0, concat_axis=0, tiled=True)
    return before.reshape(-1, HD, HD)


def attention(
    place, incoming, queries, key_rows, value_rows, out_gate, log_decay, attn_gain, out_weight, hidden_in, meta
):
    heads = log_decay.shape[0]
    block = queries.shape[0]
    width = out_weight.shape[1]
    tile = 768
    whole = lambda *shape: pl.BlockSpec(shape, lambda i, p: (0,) * len(shape))
    shapes = [(SIDE, 64, width // SIDE + 128), (SIDE, 64, width // SIDE)]
    return pl.pallas_call(
        mix_kernel,
        grid_spec=pltpu.PrefetchScalarGridSpec(
            num_scalar_prefetch=1,
            grid=(1,),
            in_specs=[whole(block, heads * HD)] * 4
            + [
                whole(heads, block),
                whole(heads, HD, HD),
                whole(1, heads * HD),
                whole(*hidden_in.shape),
                whole(*meta.shape),
                pl.BlockSpec(memory_space=pltpu.HBM),
            ],
            out_specs=[whole(*shape) for shape in shapes],
            scratch_shapes=[
                pltpu.VMEM((block, heads * HD), bf16),
                pltpu.VMEM((width // tile, heads * HD, tile), bf16),
                pltpu.SemaphoreType.DMA((width // tile,)),
            ],
        ),
        out_shape=[jax.ShapeDtypeStruct(shape, bf16) for shape in shapes],
        compiler_params=pltpu.CompilerParams(vmem_limit_bytes=60 << 20),
    )(
        place, queries, key_rows, value_rows, out_gate, log_decay, incoming, attn_gain.reshape(1, -1),
        hidden_in, meta, out_weight,
    )


def cut_kernel(layout, chips, *refs):
    sources, outs, sems = refs[: sum(layout)], refs[sum(layout) : -1], refs[-1]
    copies = []
    for i, (out, count) in enumerate(zip(outs, layout)):
        part = out.shape[2]
        lanes = pl.ds(pl.multiple_of(chips[i] * part, part), part)
        for j in range(count):
            copies.append(pltpu.make_async_copy(sources[j].at[:, lanes], out.at[j], sems.at[i, j]))
            copies[-1].start()
        sources = sources[count:]
    for copy in copies:
        copy.wait()


def cut(chips, wanted, part):
    units = wanted[0][0].shape[0]
    layout = [len(arrays) for arrays in wanted]
    shapes = [(count, units, part) for count in layout]
    outs = pl.pallas_call(
        functools.partial(cut_kernel, layout),
        grid_spec=pltpu.PrefetchScalarGridSpec(
            num_scalar_prefetch=1,
            grid=(1,),
            in_specs=[pl.BlockSpec(memory_space=pltpu.HBM)] * sum(layout),
            out_specs=[pl.BlockSpec(shape, lambda t, chips: (0, 0, 0)) for shape in shapes],
            scratch_shapes=[pltpu.SemaphoreType.DMA((len(layout), max(layout)))],
        ),
        out_shape=[jax.ShapeDtypeStruct(shape, bf16) for shape in shapes],
        compiler_params=pltpu.CompilerParams(vmem_limit_bytes=60 << 20),
    )(chips, *[array for arrays in wanted for array in arrays])
    return [out.reshape(-1, part) for out in outs]


def parts_of(refs, first, count):
    found, base, done = [], 0, 0
    for ref, begin, length in refs:
        low, high = max(first, base), min(first + count, base + length)
        if low < high:
            found.append((ref, begin + low - base, high - low, done))
            done += high - low
        base += length
    return found


def gate_up_kernel(layout, units, ids, *refs):
    x_count, holds, done = layout
    x_refs, refs = refs[:x_count], refs[x_count:]
    done_refs, refs = refs[:done], refs[done:]
    pieces = []
    for begins in holds:
        n = len(begins)
        pieces.append([(ref, begin, 2 * units // n) for ref, begin in zip(refs[:n], begins)])
        refs = refs[n:]
    out_ref, buffer, rows, acc, tails, sems, x_sems, done_sem = refs
    kept = 0
    for ref in done_refs:
        kept = ref.shape[1]
        done_copy = pltpu.make_async_copy(ref, out_ref.at[:, pl.ds(0, kept)], done_sem)
        done_copy.start()
    depth = buffer.shape[2]
    x_copies = []
    start = 0
    for i, ref in enumerate(x_refs):
        for j in range(ref.shape[0]):
            copy = pltpu.make_async_copy(ref.at[j], rows.at[pl.ds(start, 64)], x_sems.at[i, j])
            copy.start()
            x_copies.append(copy)
            start += 64
    wide = 2 * units
    edge = wide // 128 * 128
    rest = wide - edge
    copies = []
    for i, arrays in enumerate(pieces):
        pair, which = i // 2, i % 2
        moves = []
        for first, count, there in ((0, edge, which * edge), (edge, rest, 2 * edge + which * rest)):
            for ref, low, n, before in parts_of(arrays, first, count):
                moves.append((ref.at[pl.ds(low, n)], buffer.at[pair, pl.ds(there + before, n)]))
        copies.append([])
        for j, (source, target) in enumerate(moves):
            copy = pltpu.make_async_copy(source, target, sems.at[i, j])
            copy.start()
            copies[-1].append(copy)
    total = rows.shape[0]
    for copy in x_copies:
        copy.wait()
    tile = 256
    for pair in range(len(pieces) // 2):
        for which in range(2):
            for copy in copies[2 * pair + which]:
                copy.wait()
        experts = [ids[2 + 2 * pair + which].astype(f32) for which in range(2)]

        @pl.loop(0, total // tile)
        def _(t):
            at = pl.ds(pl.multiple_of(t * tile, tile), tile)
            part = dot_nt(rows[at, :depth], buffer[pair])
            meta = rows[at, depth:].astype(f32)
            last = part[:, 2 * edge :]
            turned = pltpu.roll(last, rest, 1)
            for k in range(2):
                named = [meta[:, 64 + k : 65 + k] == expert for expert in experts]
                acc[k, at] = jnp.where(
                    named[0], part[:, :edge], jnp.where(named[1], part[:, edge : 2 * edge], acc[k, at])
                )
                tails[k, at] = jnp.where(named[0], last, jnp.where(named[1], turned, tails[k, at]))

    @pl.loop(0, total // tile)
    def _(t):
        at = pl.ds(pl.multiple_of(t * tile, tile), tile)
        lane = lax.broadcasted_iota(jnp.int32, (tile, 128), 1)
        for k in range(2):
            last = jnp.where(lane < rest, tails[k, at], rows[at, depth:].astype(f32)).astype(bf16)
            head = acc[k, at].astype(bf16)
            lanes = k * (edge + 128)
            for i in range(SIDE):
                rel = lax.rem(i + SIDE - ids[0], SIDE)
                cut = slice(i * 64, i * 64 + 64)
                out_ref[rel, kept + t, :, lanes : lanes + edge] = head[cut]
                out_ref[rel, kept + t, :, lanes + edge : lanes + edge + 128] = last[cut]

    if kept:
        done_copy.wait()


def gate_up(ids, xs, pieces, units, done=()):
    blocks = sum(x.shape[0] for x in xs)
    depth = pieces[0][0][0].shape[1]
    edge = 2 * units // 128 * 128
    whole = lambda shape: pl.BlockSpec(shape, lambda i, p: (0,) * len(shape))
    kept = sum(y.shape[1] for y in done)
    shape = (SIDE, kept + blocks // SIDE, 64, 2 * (edge + 128))
    flat = [array for arrays in pieces for array, _ in arrays]
    return pl.pallas_call(
        functools.partial(gate_up_kernel, (len(xs), [[begin for _, begin in arrays] for arrays in pieces], len(done)), units),
        grid_spec=pltpu.PrefetchScalarGridSpec(
            num_scalar_prefetch=1,
            grid=(1,),
            in_specs=[pl.BlockSpec(memory_space=pl.ANY)] * (len(xs) + len(done))
            + [pl.BlockSpec(memory_space=pltpu.HBM)] * len(flat),
            out_specs=whole(shape),
            scratch_shapes=[
                pltpu.VMEM((len(pieces) // 2, 4 * units, depth), bf16),
                pltpu.VMEM((blocks * 64, xs[0].shape[2]), bf16),
                pltpu.VMEM((2, blocks * 64, edge), f32),
                pltpu.VMEM((2, blocks * 64, 128), f32),
                pltpu.SemaphoreType.DMA((len(pieces), 4)),
                pltpu.SemaphoreType.DMA((len(xs), SIDE)),
                pltpu.SemaphoreType.DMA,
            ],
        ),
        out_shape=jax.ShapeDtypeStruct(shape, bf16),
        cost_estimate=pl.CostEstimate(
            flops=2 * blocks * 64 * depth * units * 16, bytes_accessed=20 << 20, transcendentals=0
        ),
        compiler_params=pltpu.CompilerParams(vmem_limit_bytes=34 << 20),
    )(ids, *xs, *done, *flat)


def down_kernel(layout, units, ids, *refs):
    h_count, firsts = layout
    h_refs, pieces, (out_ref, buffer, spread, sems) = refs[:h_count], refs[h_count:-4], refs[-4:]
    pad = buffer.shape[1]
    copies = []
    tile = 512
    for n in range(buffer.shape[2] // tile):
        lanes = pl.ds(n * tile, tile)
        copies.append([])
        for i, (ref, first) in enumerate(zip(pieces, firsts)):
            copy = pltpu.make_async_copy(
                ref.at[pl.ds(first, units), lanes], buffer.at[i, pl.ds(0, units), lanes], sems.at[n, i]
            )
            copy.start()
            copies[-1].append(copy)
    groups = h_refs[0].shape[0]
    rows = groups * 64
    for j, ref in enumerate(h_refs):
        h = ref[...].reshape(rows, ref.shape[2]).astype(f32)
        first = h[:, 2 * units : 2 * units + 1]
        second = h[:, 2 * units + 1 : 2 * units + 2]
        turned = pltpu.roll(h, h.shape[1] - units, 1)[:, :pad]
        for i in range(8):
            expert = ids[2 + i].astype(f32)
            kept = jnp.where(first == expert, h[:, :pad], jnp.where(second == expert, turned, 0.0))
            spread[j * rows : j * rows + rows, i * pad : i * pad + pad] = kept.astype(bf16)
    for i in range(8):
        buffer[i, units:, :] = jnp.zeros((pad - units, buffer.shape[2]), bf16)
    weights = buffer.reshape(8 * pad, buffer.shape[2])
    for n in range(buffer.shape[2] // tile):
        lanes = pl.ds(n * tile, tile)
        for copy in copies[n]:
            copy.wait()
        result = jnp.dot(spread[...], weights[:, lanes], preferred_element_type=f32).astype(bf16)
        for j in range(h_count):
            for g in range(groups):
                first = j * rows + g * 64
                out_ref[g, ids[10 + j], :, lanes] = result[first : first + 64]


def down(ids, hidden, pieces, firsts, units):
    width = pieces[0].shape[1]
    pad = units + -units % 128
    groups = hidden[0].shape[0]
    shape = (groups, SIDE, 64, width)
    whole = lambda shape: pl.BlockSpec(shape, lambda i, p: (0,) * len(shape))
    return pl.pallas_call(
        functools.partial(down_kernel, (len(hidden), firsts), units),
        grid_spec=pltpu.PrefetchScalarGridSpec(
            num_scalar_prefetch=1,
            grid=(1,),
            in_specs=[whole(h.shape) for h in hidden] + [pl.BlockSpec(memory_space=pltpu.HBM)] * 8,
            out_specs=whole(shape),
            scratch_shapes=[
                pltpu.VMEM((8, pad, width), bf16),
                pltpu.VMEM((groups * SIDE * 64, 8 * pad), bf16),
                pltpu.SemaphoreType.DMA((width // 512, 8)),
            ],
        ),
        out_shape=jax.ShapeDtypeStruct(shape, bf16),
        cost_estimate=pl.CostEstimate(
            flops=2 * groups * 4 * 64 * 8 * pad * width, bytes_accessed=12 << 20, transcendentals=0
        ),
        compiler_params=pltpu.CompilerParams(vmem_limit_bytes=32 << 20),
    )(ids, *hidden, *pieces)


def fan(value, perm):
    far = send(value, perm(2))
    return send(value, perm(1)), send(value, perm(-1)), far


def plus(a, b):
    return (a.astype(f32) + b.astype(f32)).astype(bf16)


def deliver(behind, ahead, far, perm):
    far = send(far, perm(2))
    got = send(ahead, perm(1)), send(behind, perm(-1)), far
    return got[0].astype(f32) + got[1].astype(f32) + got[2].astype(f32)


def after(value, *others):
    return lax.optimization_barrier((value, others))[0]


def fetch_sum(own, behind, ahead, far, perm):
    far = send(far, perm(2))
    return [own, send(ahead, perm(1)), send(behind, perm(-1)), far]


def join_kernel(own, right, left, far, gain_ref, rows_ref, mid_ref):
    part = mid_ref.shape[1]
    total = own[...].astype(f32) + right[...].astype(f32) + left[...].astype(f32) + far[...].astype(f32)
    mid = total[:, :part].astype(bf16)
    mid_ref[...] = mid
    mid = mid.astype(f32)
    rows_ref[:, :part] = (mid * gain_ref[...]).astype(bf16)
    squares = jnp.sum(mid * mid, axis=1, keepdims=True)
    high = squares.astype(bf16).astype(f32)
    lane = lax.broadcasted_iota(jnp.int32, (rows_ref.shape[0], 128), 1)
    tail = jnp.where(lane == 72, high, jnp.where(lane == 73, squares - high, total[:, part:]))
    rows_ref[:, part:] = tail.astype(bf16)


def join(values, gain):
    count, width = values[0].shape
    return pl.pallas_call(
        join_kernel,
        out_shape=[jax.ShapeDtypeStruct((count, n), bf16) for n in (width, width - 128)],
        compiler_params=pltpu.CompilerParams(vmem_limit_bytes=8 << 20),
    )(*values, gain.reshape(1, -1))


def activate_kernel(units, width, own, right, left, far, out_ref):
    total = own[...].astype(f32) + right[...].astype(f32) + left[...].astype(f32) + far[...].astype(f32)
    total = total.reshape(-1, total.shape[2])
    col = total.shape[1] // 2
    wide = 2 * units
    scale = lax.rsqrt((total[:, wide + 8 : wide + 9] + total[:, wide + 9 : wide + 10]) / width + 1e-06)
    lane = lax.broadcasted_iota(jnp.int32, (total.shape[0], col), 1)
    result = []
    for k in range(2):
        gate = total[:, k * col : k * col + col] * scale
        up = pltpu.roll(gate, col - units, 1)
        at = wide + 2 + 3 * k
        weight = total[:, at : at + 1] + total[:, at + 1 : at + 2] + total[:, at + 2 : at + 3]
        result.append(gate / (1.0 + jnp.exp(-gate)) * up * (weight * (1.0 / SIDE)))
    value = jnp.where(lane < units, result[0], pltpu.roll(result[1], units, 1))
    value = jnp.where(lane < wide, value, 0.0)
    for j in range(2):
        route = total[:, wide + j : wide + j + 1] * (1.0 / SIDE)
        value = jnp.where(lane == wide + j, route, value)
    out_ref[...] = value.astype(bf16).reshape(out_ref.shape)


def activate(values, units, width):
    return pl.pallas_call(
        functools.partial(activate_kernel, units, width),
        out_shape=jax.ShapeDtypeStruct(values[0].shape[:2] + (values[0].shape[2] // 2,), bf16),
        compiler_params=pltpu.CompilerParams(vmem_limit_bytes=24 << 20),
    )(*values)


def per_device(
    hidden_in,
    queries,
    key_rows,
    value_rows,
    out_gate,
    log_decay,
    attn_gain,
    out_weight,
    ffn_gain,
    routes,
    combine_weight,
    gate_weight,
    up_weight,
    down_weight,
):
    width = hidden_in.shape[1]
    part = width // SIDE
    units = gate_weight.shape[2]
    at = lax.axis_index("exp")
    x, core = at // CORES, lax.rem(at, CORES)
    order = [0, -1, 1, 2]
    chips = [lax.rem(x + d + SIDE, SIDE) for d in order]
    place = jnp.stack(
        [x, core]
        + [e for chip in chips for e in (2 * chip + core, 2 * chip + 1 - core)]
        + chips
    ).astype(jnp.int32)

    gate_t, up_t, down_w = gate_weight[0].T, up_weight[0].T, down_weight[0]

    at_chip = lambda *ds: jnp.stack([lax.rem(x + d + SIDE, SIDE) for d in ds]).astype(jnp.int32)
    gate_up_t = [gate_t, up_t]

    to_ahead, to_behind = cut(at_chip(1, -1), [[gate_t], [gate_t]], part)
    key_rows, to_ahead, to_behind = lax.optimization_barrier((key_rows, to_ahead, to_behind))
    g_behind, g_ahead = send(to_ahead, along_x(1)), send(to_behind, along_x(-1))

    toks = hidden_in.shape[0]
    routes_f = routes.astype(f32)
    cw = split3(combine_weight)
    lanes = [routes_f[:, 0:1], routes_f[:, 1:2]] + [w[:, k : k + 1] for k in range(2) for w in cw]
    meta = jnp.concatenate([jnp.zeros((toks, 64), f32)] + lanes + [jnp.zeros((toks, 64 - len(lanes)), f32)], 1)
    states = block_states(key_rows, value_rows, log_decay)
    up_ahead, up_behind, far_gate, far_up, w_mine, far_down, down_ahead, down_behind = cut(
        at_chip(1, -1, 2, 2, 0, 2, 1, -1),
        [[up_t], [up_t], [gate_t], [up_t], gate_up_t + [down_w], [down_w], [down_w], [down_w]],
        part,
    )
    states, g_behind, g_ahead, up_ahead, up_behind, far_gate, far_up, w_mine = lax.optimization_barrier(
        (states, g_behind, g_ahead, up_ahead, up_behind, far_gate, far_up, w_mine)
    )
    u_behind, u_ahead = send(up_ahead, along_x(1)), send(up_behind, along_x(-1))
    g_far, u_far = send(far_gate, along_x(2)), send(far_up, along_x(2))
    s_mine = send(w_mine, OTHER_CORE)
    incoming = earlier_states(states)
    mine, other = attention(
        place, incoming, queries, key_rows, value_rows, out_gate, log_decay, attn_gain, out_weight, hidden_in,
        meta.astype(bf16),
    )
    u_behind, u_ahead, g_far, s_mine, mine, other = lax.optimization_barrier(
        (u_behind, u_ahead, g_far, s_mine, mine, other)
    )
    other = send(other, OTHER_CORE)
    summed = jnp.concatenate([plus(mine[:, :, :part], other), mine[:, :, part:]], 2)
    gain = lax.dynamic_slice(ffn_gain, (x * part,), (part,))
    values = fetch_sum(summed[0], summed[3], summed[1], summed[2], along_x)
    values, u_far, gain, far_down, down_ahead, down_behind = lax.optimization_barrier(
        (values, u_far, gain, far_down, down_ahead, down_behind)
    )
    first = jnp.concatenate([g_behind, u_behind, g_ahead, u_ahead, g_far, u_far], 0)
    rows, mid = join(values, gain)
    mid_f = mid.astype(f32)

    s_first = send(first, OTHER_CORE)
    plane = jnp.stack([rows, *fan(rows, along_first)])
    s_first, plane = lax.optimization_barrier((s_first, plane))
    right, left = send(plane, along_second(1)), send(plane, along_second(-1))
    d_behind, d_ahead = send(down_ahead, along_x(1)), send(down_behind, along_x(-1))
    d_far = send(far_down, along_x(2))
    far = send(right[:2], along_second(1)), send(left[2:], along_second(-1))
    wide = 2 * units
    weights = [((w_mine, 0),), ((s_mine, 0),), ((g_behind, 0), (u_behind, 0)), ((s_first, 0),)]
    weights += [((g_ahead, 0), (u_ahead, 0)), ((s_first, wide),), ((g_far, 0), (u_far, 0))]
    weights += [((s_first, 2 * wide),)]
    y = gate_up(place, [plane, right, left], weights, units)
    far, y = lax.optimization_barrier((far, y))
    y_last = gate_up(place, far, weights, units)
    values = fetch_sum(y[0], y[3], y[1], y[2], along_x)
    values, d_behind, d_ahead, d_far, y_last = lax.optimization_barrier(
        (values, d_behind, d_ahead, d_far, y_last)
    )
    s_down = send(jnp.concatenate([d_behind, d_ahead, d_far], 0), OTHER_CORE)
    hidden = activate(values, units, width)
    hidden = [hidden, *fan(hidden, along_x)]
    values = fetch_sum(y_last[0], y_last[3], y_last[1], y_last[2], along_x)
    hidden, s_down, values = lax.optimization_barrier((hidden, s_down, values))
    hidden_last = activate(values, units, width)
    hidden_last = [hidden_last, *fan(hidden_last, along_x)]
    down_pieces = [w_mine, s_mine, d_behind, s_down, d_ahead, s_down, d_far, s_down]
    firsts = [wide, wide, 0, 0, 0, units, 0, wide]
    out = down(place, hidden, down_pieces, firsts, units)
    got = send(out[2], along_second(1)).astype(f32) + send(out[1], along_second(-1)).astype(f32)
    last = down(place, hidden_last, down_pieces, firsts, units)
    out = out[0].astype(f32) + (got + send(last[0], along_second(2)).astype(f32))
    own = out[0]
    out = out.astype(bf16)
    out = own + deliver(out[1], out[2], out[3], along_first)
    out = (mid_f + out).astype(bf16).reshape(SIDE, toks, part)
    pick = lambda d: lax.dynamic_index_in_dim(out, chips[order.index(d)], 0, False)
    far = send(pick(2), along_x(2))
    columns = jnp.stack([pick(0), send(pick(-1), along_x(-1)), far, send(pick(1), along_x(1))])
    columns = jnp.roll(columns, x, axis=0)
    return columns.transpose(1, 0, 2).reshape(toks, width)


def solution(mesh):
    return jax.shard_map(
        per_device,
        mesh=mesh,
        in_specs=(
            P(("seq", "exp"), None),
            P("seq", "exp"),
            P("seq", "exp"),
            P("seq", "exp"),
            P("seq", "exp"),
            P("exp", "seq"),
            P("exp"),
            P("exp", None),
            P(),
            P(("seq", "exp"), None),
            P(("seq", "exp"), None),
            P("exp", None, "seq"),
            P("exp", None, "seq"),
            P("exp", "seq", None),
        ),
        out_specs=P(("seq", "exp"), None),
        check_vma=False,
    )
```

```python
import functools

import jax
import jax.numpy as jnp
from jax import lax
from jax.experimental import pallas as pl
from jax.experimental.pallas import tpu as pltpu
from jax.sharding import PartitionSpec as P

f32 = jnp.float32
bf16 = jnp.bfloat16
SIDE = 4
CORES = 2
AXES = ("seq", "exp")
HD = 128


def permutation(move):
    pairs = []
    for z in range(SIDE):
        for y in range(SIDE):
            for x in range(SIDE):
                for c in range(CORES):
                    z2, y2, x2, c2 = move(z, y, x, c)
                    source = ((z * SIDE + y) * SIDE + x) * CORES + c
                    target = (((z2 % SIDE) * SIDE + y2 % SIDE) * SIDE + x2 % SIDE) * CORES + c2
                    pairs.append((source, target))
    return pairs


def along_x(k):
    return permutation(lambda z, y, x, c: (z, y, x + k, c))


def along_first(k):
    return permutation(lambda z, y, x, c: (z, y + k, x, c) if c == 0 else (z + k, y, x, c))


def along_second(k):
    return permutation(lambda z, y, x, c: (z + k, y, x, c) if c == 0 else (z, y + k, x, c))


OTHER_CORE = permutation(lambda z, y, x, c: (z, y, x, 1 - c))


def send(value, perm):
    return lax.ppermute(value, AXES, perm)


def split3(value):
    high = lax.reduce_precision(value, 8, 7)
    rest = value - high
    mid = lax.reduce_precision(rest, 8, 7)
    return high, mid, rest - mid


def lower_triangle(n):
    row = lax.broadcasted_iota(jnp.int32, (n, n), 0)
    col = lax.broadcasted_iota(jnp.int32, (n, n), 1)
    return row >= col


def dot_nt(a, b, **kw):
    return lax.dot_general(a, b, (((1,), (1,)), ((), ())), preferred_element_type=f32, **kw)


def dot_tn(a, b, **kw):
    return lax.dot_general(a, b, (((0,), (0,)), ((), ())), preferred_element_type=f32, **kw)


def state_kernel(k_ref, v_ref, ld_ref, out_ref):
    heads, block = ld_ref.shape
    low = lower_triangle(block).astype(f32)
    ld = ld_ref[...]
    cum_col = dot_nt(low, ld, precision=lax.Precision.HIGHEST)
    ends = cum_col[block - 1 : block, :]
    factor = jnp.exp(ends - cum_col)
    rows = lax.broadcasted_iota(jnp.int32, (16, HD), 0)
    for h in range(heads):
        lanes = pl.ds(h * HD, HD)
        keyed = (k_ref[:, lanes].astype(f32) * factor[:, h : h + 1]).astype(bf16)
        state = dot_tn(keyed, v_ref[:, lanes]).astype(bf16)
        end = jnp.broadcast_to(ends[:, h : h + 1], (16, HD))
        high = end.astype(bf16).astype(f32)
        rest = end - high
        mid = rest.astype(bf16).astype(f32)
        tail = jnp.where(rows == 0, high, jnp.where(rows == 1, mid, jnp.where(rows == 2, rest - mid, 0.0)))
        tail = tail.astype(bf16)
        for part in range(2):
            out_ref[2 * h + part, 0:64, :] = state[part * 64 : part * 64 + 64]
            out_ref[2 * h + part, 64:80, :] = tail


def scan_kernel(in_ref, out_ref):
    count = in_ref.shape[0]
    carry = jnp.zeros((64, HD), f32)
    for i in range(count):
        out_ref[i] = carry.astype(bf16)
        if i + 1 < count:
            tail = in_ref[i, 64:80, :].astype(f32)
            end = tail[0:1] + tail[1:2] + tail[2:3]
            carry = jnp.exp(end) * carry + in_ref[i, 0:64, :].astype(f32)


def mix_kernel(
    place, q_ref, k_ref, v_ref, g_ref, ld_ref, inc_ref, gain_ref, hid_ref, meta_ref, w_ref,
    mine_ref, other_ref, gated, buffer, sems,
):
    heads, block = ld_ref.shape
    tiles = buffer.shape[0]
    tile = buffer.shape[2]
    copies = [
        pltpu.make_async_copy(w_ref.at[:, pl.ds(i * tile, tile)], buffer.at[i], sems.at[i]) for i in range(tiles)
    ]
    for copy in copies:
        copy.start()
    causal = lower_triangle(block)
    low = causal.astype(f32)
    ld = ld_ref[...]
    cum_col = dot_nt(low, ld, precision=lax.Precision.HIGHEST)
    cum_row = dot_nt(ld, low, precision=lax.Precision.HIGHEST)
    grown = jnp.exp(cum_col)
    for h in range(heads):
        lanes = pl.ds(h * HD, HD)
        q, k, v = q_ref[:, lanes], k_ref[:, lanes], v_ref[:, lanes]
        spread = cum_col[:, h : h + 1] - cum_row[h : h + 1, :]
        weights = jnp.where(causal, dot_nt(q, k) * jnp.exp(jnp.where(causal, spread, 0.0)), 0.0)
        intra = jnp.dot(weights.astype(bf16), v, preferred_element_type=f32)
        inter = jnp.dot(q, inc_ref[h], preferred_element_type=f32) * grown[:, h : h + 1]
        mixed = intra + inter
        normal = mixed * lax.rsqrt(jnp.mean(mixed * mixed, axis=-1, keepdims=True) + 1e-05)
        gate = 1.0 / (1.0 + jnp.exp(-g_ref[:, lanes].astype(f32)))
        result = (normal * gain_ref[:, lanes] * gate).astype(bf16)
        for x in range(SIDE):
            for c in range(CORES):
                there = pl.multiple_of(lax.rem(c + place[1], CORES) * 64 + x * 16, 16)
                gated[pl.ds(there, 16), lanes] = result[x * 32 + c * 16 : x * 32 + c * 16 + 16]
    toks = hid_ref.shape[0]
    own = pl.ds(pl.multiple_of(place[0] * toks, toks), toks)
    per = tiles // SIDE
    width = per * tile
    for rel in range(SIDE):
        mine_ref[rel, :, width:] = jnp.zeros((64, 128), bf16)
        mine_ref[rel, own, width:] = meta_ref[...]
    for i in range(tiles):
        copies[i].wait()
        rel = lax.rem(i // per + SIDE - place[0], SIDE)
        lanes = pl.ds(i % per * tile, tile)
        product = jnp.dot(gated[...], buffer[i], preferred_element_type=f32)
        mine_ref[rel, :, lanes] = product[:64].astype(bf16)
        again = mine_ref[rel, own, lanes].astype(f32) + hid_ref[:, i * tile : i * tile + tile].astype(f32)
        mine_ref[rel, own, lanes] = again.astype(bf16)
        other_ref[rel, :, lanes] = product[64:].astype(bf16)


def block_states(key_rows, value_rows, log_decay):
    heads = log_decay.shape[0]
    pieces = pl.pallas_call(
        state_kernel,
        out_shape=jax.ShapeDtypeStruct((2 * heads, 80, HD), bf16),
        compiler_params=pltpu.CompilerParams(vmem_limit_bytes=16 << 20),
    )(key_rows, value_rows, log_decay)
    return lax.all_to_all(pieces, "seq", split_axis=0, concat_axis=0, tiled=True)


def earlier_states(pieces):
    before = pl.pallas_call(
        scan_kernel,
        out_shape=jax.ShapeDtypeStruct((pieces.shape[0], 64, HD), bf16),
        compiler_params=pltpu.CompilerParams(vmem_limit_bytes=16 << 20),
    )(pieces)
    before = lax.all_to_all(before, "seq", split_axis=0, concat_axis=0, tiled=True)
    return before.reshape(-1, HD, HD)


def attention(
    place, incoming, queries, key_rows, value_rows, out_gate, log_decay, attn_gain, out_weight, hidden_in, meta
):
    heads = log_decay.shape[0]
    block = queries.shape[0]
    width = out_weight.shape[1]
    tile = 768
    whole = lambda *shape: pl.BlockSpec(shape, lambda i, p: (0,) * len(shape))
    shapes = [(SIDE, 64, width // SIDE + 128), (SIDE, 64, width // SIDE)]
    return pl.pallas_call(
        mix_kernel,
        grid_spec=pltpu.PrefetchScalarGridSpec(
            num_scalar_prefetch=1,
            grid=(1,),
            in_specs=[whole(block, heads * HD)] * 4
            + [
                whole(heads, block),
                whole(heads, HD, HD),
                whole(1, heads * HD),
                whole(*hidden_in.shape),
                whole(*meta.shape),
                pl.BlockSpec(memory_space=pltpu.HBM),
            ],
            out_specs=[whole(*shape) for shape in shapes],
            scratch_shapes=[
                pltpu.VMEM((block, heads * HD), bf16),
                pltpu.VMEM((width // tile, heads * HD, tile), bf16),
                pltpu.SemaphoreType.DMA((width // tile,)),
            ],
        ),
        out_shape=[jax.ShapeDtypeStruct(shape, bf16) for shape in shapes],
        compiler_params=pltpu.CompilerParams(vmem_limit_bytes=60 << 20),
    )(
        place, queries, key_rows, value_rows, out_gate, log_decay, incoming, attn_gain.reshape(1, -1),
        hidden_in, meta, out_weight,
    )


def cut_kernel(layout, chips, *refs):
    sources, outs, sems = refs[: sum(layout)], refs[sum(layout) : -1], refs[-1]
    copies = []
    for i, (out, count) in enumerate(zip(outs, layout)):
        part = out.shape[2]
        lanes = pl.ds(pl.multiple_of(chips[i] * part, part), part)
        for j in range(count):
            copies.append(pltpu.make_async_copy(sources[j].at[:, lanes], out.at[j], sems.at[i, j]))
            copies[-1].start()
        sources = sources[count:]
    for copy in copies:
        copy.wait()


def cut(chips, wanted, part):
    units = wanted[0][0].shape[0]
    layout = [len(arrays) for arrays in wanted]
    shapes = [(count, units, part) for count in layout]
    outs = pl.pallas_call(
        functools.partial(cut_kernel, layout),
        grid_spec=pltpu.PrefetchScalarGridSpec(
            num_scalar_prefetch=1,
            grid=(1,),
            in_specs=[pl.BlockSpec(memory_space=pltpu.HBM)] * sum(layout),
            out_specs=[pl.BlockSpec(shape, lambda t, chips: (0, 0, 0)) for shape in shapes],
            scratch_shapes=[pltpu.SemaphoreType.DMA((len(layout), max(layout)))],
        ),
        out_shape=[jax.ShapeDtypeStruct(shape, bf16) for shape in shapes],
        compiler_params=pltpu.CompilerParams(vmem_limit_bytes=60 << 20),
    )(chips, *[array for arrays in wanted for array in arrays])
    return [out.reshape(-1, part) for out in outs]


def parts_of(refs, first, count):
    found, base, done = [], 0, 0
    for ref, begin, length in refs:
        low, high = max(first, base), min(first + count, base + length)
        if low < high:
            found.append((ref, begin + low - base, high - low, done))
            done += high - low
        base += length
    return found


def gate_up_kernel(layout, units, ids, *refs):
    x_count, holds, done = layout
    x_refs, refs = refs[:x_count], refs[x_count:]
    done_refs, refs = refs[:done], refs[done:]
    pieces = []
    for begins in holds:
        n = len(begins)
        pieces.append([(ref, begin, 2 * units // n) for ref, begin in zip(refs[:n], begins)])
        refs = refs[n:]
    out_ref, buffer, rows, acc, tails, sems, x_sems, done_sem = refs
    kept = 0
    for ref in done_refs:
        kept = ref.shape[1]
        done_copy = pltpu.make_async_copy(ref, out_ref.at[:, pl.ds(0, kept)], done_sem)
        done_copy.start()
    depth = buffer.shape[2]
    x_copies = []
    start = 0
    for i, ref in enumerate(x_refs):
        for j in range(ref.shape[0]):
            copy = pltpu.make_async_copy(ref.at[j], rows.at[pl.ds(start, 64)], x_sems.at[i, j])
            copy.start()
            x_copies.append(copy)
            start += 64
    wide = 2 * units
    edge = wide // 128 * 128
    rest = wide - edge
    copies = []
    for i, arrays in enumerate(pieces):
        pair, which = i // 2, i % 2
        moves = []
        for first, count, there in ((0, edge, which * edge), (edge, rest, 2 * edge + which * rest)):
            for ref, low, n, before in parts_of(arrays, first, count):
                moves.append((ref.at[pl.ds(low, n)], buffer.at[pair, pl.ds(there + before, n)]))
        copies.append([])
        for j, (source, target) in enumerate(moves):
            copy = pltpu.make_async_copy(source, target, sems.at[i, j])
            copy.start()
            copies[-1].append(copy)
    total = rows.shape[0]
    for copy in x_copies:
        copy.wait()
    tile = 384 if total % 384 == 0 else 256
    for pair in range(len(pieces) // 2):
        for which in range(2):
            for copy in copies[2 * pair + which]:
                copy.wait()
        experts = [ids[2 + 2 * pair + which].astype(f32) for which in range(2)]

        @pl.loop(0, total // tile)
        def _(t):
            at = pl.ds(pl.multiple_of(t * tile, tile), tile)
            part = dot_nt(rows[at, :depth], buffer[pair])
            meta = rows[at, depth:].astype(f32)
            last = part[:, 2 * edge :]
            turned = pltpu.roll(last, rest, 1)
            for k in range(2):
                named = [meta[:, 64 + k : 65 + k] == expert for expert in experts]
                acc[k, at] = jnp.where(
                    named[0], part[:, :edge], jnp.where(named[1], part[:, edge : 2 * edge], acc[k, at])
                )
                tails[k, at] = jnp.where(named[0], last, jnp.where(named[1], turned, tails[k, at]))

    tile = 256

    @pl.loop(0, total // tile)
    def _(t):
        at = pl.ds(pl.multiple_of(t * tile, tile), tile)
        lane = lax.broadcasted_iota(jnp.int32, (tile, 128), 1)
        for k in range(2):
            last = jnp.where(lane < rest, tails[k, at], rows[at, depth:].astype(f32)).astype(bf16)
            head = acc[k, at].astype(bf16)
            lanes = k * (edge + 128)
            for i in range(SIDE):
                rel = lax.rem(i + SIDE - ids[0], SIDE)
                cut = slice(i * 64, i * 64 + 64)
                out_ref[rel, kept + t, :, lanes : lanes + edge] = head[cut]
                out_ref[rel, kept + t, :, lanes + edge : lanes + edge + 128] = last[cut]

    if kept:
        done_copy.wait()


def gate_up(ids, xs, pieces, units, done=()):
    blocks = sum(x.shape[0] for x in xs)
    depth = pieces[0][0][0].shape[1]
    edge = 2 * units // 128 * 128
    whole = lambda shape: pl.BlockSpec(shape, lambda i, p: (0,) * len(shape))
    kept = sum(y.shape[1] for y in done)
    shape = (SIDE, kept + blocks // SIDE, 64, 2 * (edge + 128))
    flat = [array for arrays in pieces for array, _ in arrays]
    return pl.pallas_call(
        functools.partial(gate_up_kernel, (len(xs), [[begin for _, begin in arrays] for arrays in pieces], len(done)), units),
        grid_spec=pltpu.PrefetchScalarGridSpec(
            num_scalar_prefetch=1,
            grid=(1,),
            in_specs=[pl.BlockSpec(memory_space=pl.ANY)] * (len(xs) + len(done))
            + [pl.BlockSpec(memory_space=pltpu.HBM)] * len(flat),
            out_specs=whole(shape),
            scratch_shapes=[
                pltpu.VMEM((len(pieces) // 2, 4 * units, depth), bf16),
                pltpu.VMEM((blocks * 64, xs[0].shape[2]), bf16),
                pltpu.VMEM((2, blocks * 64, edge), f32),
                pltpu.VMEM((2, blocks * 64, 128), f32),
                pltpu.SemaphoreType.DMA((len(pieces), 4)),
                pltpu.SemaphoreType.DMA((len(xs), SIDE)),
                pltpu.SemaphoreType.DMA,
            ],
        ),
        out_shape=jax.ShapeDtypeStruct(shape, bf16),
        cost_estimate=pl.CostEstimate(
            flops=2 * blocks * 64 * depth * units * 16, bytes_accessed=20 << 20, transcendentals=0
        ),
        compiler_params=pltpu.CompilerParams(vmem_limit_bytes=34 << 20),
    )(ids, *xs, *done, *flat)


def down_kernel(layout, units, ids, *refs):
    h_count, firsts = layout
    h_refs, pieces, (out_ref, buffer, spread, sems) = refs[:h_count], refs[h_count:-4], refs[-4:]
    pad = buffer.shape[1]
    copies = []
    tile = 512
    for n in range(buffer.shape[2] // tile):
        lanes = pl.ds(n * tile, tile)
        copies.append([])
        for i, (ref, first) in enumerate(zip(pieces, firsts)):
            copy = pltpu.make_async_copy(
                ref.at[pl.ds(first, units), lanes], buffer.at[i, pl.ds(0, units), lanes], sems.at[n, i]
            )
            copy.start()
            copies[-1].append(copy)
    groups = h_refs[0].shape[0]
    rows = groups * 64
    for j, ref in enumerate(h_refs):
        h = ref[...].reshape(rows, ref.shape[2]).astype(f32)
        first = h[:, 2 * units : 2 * units + 1]
        second = h[:, 2 * units + 1 : 2 * units + 2]
        turned = pltpu.roll(h, h.shape[1] - units, 1)[:, :pad]
        for i in range(8):
            expert = ids[2 + i].astype(f32)
            kept = jnp.where(first == expert, h[:, :pad], jnp.where(second == expert, turned, 0.0))
            spread[j * rows : j * rows + rows, i * pad : i * pad + pad] = kept.astype(bf16)
    for i in range(8):
        buffer[i, units:, :] = jnp.zeros((pad - units, buffer.shape[2]), bf16)
    weights = buffer.reshape(8 * pad, buffer.shape[2])
    for n in range(buffer.shape[2] // tile):
        lanes = pl.ds(n * tile, tile)
        for copy in copies[n]:
            copy.wait()
        result = jnp.dot(spread[...], weights[:, lanes], preferred_element_type=f32).astype(bf16)
        for j in range(h_count):
            for g in range(groups):
                first = j * rows + g * 64
                out_ref[g, ids[10 + j], :, lanes] = result[first : first + 64]


def down(ids, hidden, pieces, firsts, units):
    width = pieces[0].shape[1]
    pad = units + -units % 128
    groups = hidden[0].shape[0]
    shape = (groups, SIDE, 64, width)
    whole = lambda shape: pl.BlockSpec(shape, lambda i, p: (0,) * len(shape))
    return pl.pallas_call(
        functools.partial(down_kernel, (len(hidden), firsts), units),
        grid_spec=pltpu.PrefetchScalarGridSpec(
            num_scalar_prefetch=1,
            grid=(1,),
            in_specs=[whole(h.shape) for h in hidden] + [pl.BlockSpec(memory_space=pltpu.HBM)] * 8,
            out_specs=whole(shape),
            scratch_shapes=[
                pltpu.VMEM((8, pad, width), bf16),
                pltpu.VMEM((groups * SIDE * 64, 8 * pad), bf16),
                pltpu.SemaphoreType.DMA((width // 512, 8)),
            ],
        ),
        out_shape=jax.ShapeDtypeStruct(shape, bf16),
        cost_estimate=pl.CostEstimate(
            flops=2 * groups * 4 * 64 * 8 * pad * width, bytes_accessed=12 << 20, transcendentals=0
        ),
        compiler_params=pltpu.CompilerParams(vmem_limit_bytes=32 << 20),
    )(ids, *hidden, *pieces)


def fan(value, perm):
    far = send(value, perm(2))
    return send(value, perm(1)), send(value, perm(-1)), far


def plus(a, b):
    return (a.astype(f32) + b.astype(f32)).astype(bf16)


def deliver(behind, ahead, far, perm):
    far = send(far, perm(2))
    got = send(ahead, perm(1)), send(behind, perm(-1)), far
    return got[0].astype(f32) + got[1].astype(f32) + got[2].astype(f32)


def after(value, *others):
    return lax.optimization_barrier((value, others))[0]


def fetch_sum(own, behind, ahead, far, perm):
    far = send(far, perm(2))
    return [own, send(ahead, perm(1)), send(behind, perm(-1)), far]


def join_kernel(own, right, left, far, gain_ref, rows_ref, mid_ref):
    part = mid_ref.shape[1]
    total = own[...].astype(f32) + right[...].astype(f32) + left[...].astype(f32) + far[...].astype(f32)
    mid = total[:, :part].astype(bf16)
    mid_ref[...] = mid
    mid = mid.astype(f32)
    rows_ref[:, :part] = (mid * gain_ref[...]).astype(bf16)
    squares = jnp.sum(mid * mid, axis=1, keepdims=True)
    high = squares.astype(bf16).astype(f32)
    lane = lax.broadcasted_iota(jnp.int32, (rows_ref.shape[0], 128), 1)
    tail = jnp.where(lane == 72, high, jnp.where(lane == 73, squares - high, total[:, part:]))
    rows_ref[:, part:] = tail.astype(bf16)


def join(values, gain):
    count, width = values[0].shape
    return pl.pallas_call(
        join_kernel,
        out_shape=[jax.ShapeDtypeStruct((count, n), bf16) for n in (width, width - 128)],
        compiler_params=pltpu.CompilerParams(vmem_limit_bytes=8 << 20),
    )(*values, gain.reshape(1, -1))


def activate_kernel(units, width, own, right, left, far, out_ref):
    total = own[...].astype(f32) + right[...].astype(f32) + left[...].astype(f32) + far[...].astype(f32)
    total = total.reshape(-1, total.shape[2])
    col = total.shape[1] // 2
    wide = 2 * units
    scale = lax.rsqrt((total[:, wide + 8 : wide + 9] + total[:, wide + 9 : wide + 10]) / width + 1e-06)
    lane = lax.broadcasted_iota(jnp.int32, (total.shape[0], col), 1)
    result = []
    for k in range(2):
        gate = total[:, k * col : k * col + col] * scale
        up = pltpu.roll(gate, col - units, 1)
        at = wide + 2 + 3 * k
        weight = total[:, at : at + 1] + total[:, at + 1 : at + 2] + total[:, at + 2 : at + 3]
        result.append(gate / (1.0 + jnp.exp(-gate)) * up * (weight * (1.0 / SIDE)))
    value = jnp.where(lane < units, result[0], pltpu.roll(result[1], units, 1))
    value = jnp.where(lane < wide, value, 0.0)
    for j in range(2):
        route = total[:, wide + j : wide + j + 1] * (1.0 / SIDE)
        value = jnp.where(lane == wide + j, route, value)
    out_ref[...] = value.astype(bf16).reshape(out_ref.shape)


def activate(values, units, width):
    return pl.pallas_call(
        functools.partial(activate_kernel, units, width),
        out_shape=jax.ShapeDtypeStruct(values[0].shape[:2] + (values[0].shape[2] // 2,), bf16),
        compiler_params=pltpu.CompilerParams(vmem_limit_bytes=24 << 20),
    )(*values)


def per_device(
    hidden_in,
    queries,
    key_rows,
    value_rows,
    out_gate,
    log_decay,
    attn_gain,
    out_weight,
    ffn_gain,
    routes,
    combine_weight,
    gate_weight,
    up_weight,
    down_weight,
):
    width = hidden_in.shape[1]
    part = width // SIDE
    units = gate_weight.shape[2]
    at = lax.axis_index("exp")
    x, core = at // CORES, lax.rem(at, CORES)
    order = [0, -1, 1, 2]
    chips = [lax.rem(x + d + SIDE, SIDE) for d in order]
    place = jnp.stack(
        [x, core]
        + [e for chip in chips for e in (2 * chip + core, 2 * chip + 1 - core)]
        + chips
    ).astype(jnp.int32)

    gate_t, up_t, down_w = gate_weight[0].T, up_weight[0].T, down_weight[0]

    at_chip = lambda *ds: jnp.stack([lax.rem(x + d + SIDE, SIDE) for d in ds]).astype(jnp.int32)
    gate_up_t = [gate_t, up_t]

    to_ahead, to_behind = cut(at_chip(1, -1), [[gate_t], [gate_t]], part)
    key_rows, to_ahead, to_behind = lax.optimization_barrier((key_rows, to_ahead, to_behind))
    g_behind, g_ahead = send(to_ahead, along_x(1)), send(to_behind, along_x(-1))

    toks = hidden_in.shape[0]
    routes_f = routes.astype(f32)
    cw = split3(combine_weight)
    lanes = [routes_f[:, 0:1], routes_f[:, 1:2]] + [w[:, k : k + 1] for k in range(2) for w in cw]
    meta = jnp.concatenate([jnp.zeros((toks, 64), f32)] + lanes + [jnp.zeros((toks, 64 - len(lanes)), f32)], 1)
    states = block_states(key_rows, value_rows, log_decay)
    up_ahead, up_behind, far_gate, w_mine, far_up, far_down, down_ahead, down_behind = cut(
        at_chip(1, -1, 2, 0, 2, 2, 1, -1),
        [[up_t], [up_t], [gate_t], gate_up_t + [down_w], [up_t], [down_w], [down_w], [down_w]],
        part,
    )
    states, g_behind, g_ahead, up_ahead, up_behind, far_gate, w_mine = lax.optimization_barrier(
        (states, g_behind, g_ahead, up_ahead, up_behind, far_gate, w_mine)
    )
    u_behind, u_ahead = send(up_ahead, along_x(1)), send(up_behind, along_x(-1))
    g_far = send(far_gate, along_x(2))
    s_mine = send(w_mine, OTHER_CORE)
    incoming = earlier_states(states)
    mine, other = attention(
        place, incoming, queries, key_rows, value_rows, out_gate, log_decay, attn_gain, out_weight, hidden_in,
        meta.astype(bf16),
    )
    u_behind, u_ahead, g_far, s_mine, mine, other = lax.optimization_barrier(
        (u_behind, u_ahead, g_far, s_mine, mine, other)
    )
    other = send(other, OTHER_CORE)
    summed = jnp.concatenate([plus(mine[:, :, :part], other), mine[:, :, part:]], 2)
    first = jnp.concatenate([g_behind, u_behind, g_ahead, u_ahead, g_far], 0)
    gain = lax.dynamic_slice(ffn_gain, (x * part,), (part,))
    values = fetch_sum(summed[0], summed[3], summed[1], summed[2], along_x)
    values, first, gain, far_up = lax.optimization_barrier((values, first, gain, far_up))
    rows, mid = join(values, gain)
    mid_f = mid.astype(f32)

    w_up = send(far_up, along_x(2))
    s_first = send(first, OTHER_CORE)
    plane = jnp.stack([rows, *fan(rows, along_first)])
    s_first, plane = lax.optimization_barrier((s_first, plane))
    right, left = send(plane, along_second(1)), send(plane, along_second(-1))
    w_up, right, left, down_ahead, down_behind, far_down = lax.optimization_barrier(
        (w_up, right, left, down_ahead, down_behind, far_down)
    )
    s_up = send(w_up, OTHER_CORE)
    far = send(right[:2], along_second(1)), send(left[2:], along_second(-1))
    d_behind, d_ahead = send(down_ahead, along_x(1)), send(down_behind, along_x(-1))
    d_far = send(far_down, along_x(2))
    wide = 2 * units
    weights = [((w_mine, 0),), ((s_mine, 0),), ((g_behind, 0), (u_behind, 0)), ((s_first, 0),)]
    weights += [((g_ahead, 0), (u_ahead, 0)), ((s_first, wide),), ((g_far, 0), (w_up, 0))]
    weights += [((s_first, 2 * wide), (s_up, 0))]
    y = gate_up(place, [plane, right, left], weights, units)
    far, y = lax.optimization_barrier((far, y))
    y_last = gate_up(place, far, weights, units)
    values = fetch_sum(y[0], y[3], y[1], y[2], along_x)
    values, d_behind, d_ahead, d_far, y_last = lax.optimization_barrier(
        (values, d_behind, d_ahead, d_far, y_last)
    )
    s_down = send(jnp.concatenate([d_behind, d_ahead, d_far], 0), OTHER_CORE)
    hidden = activate(values, units, width)
    hidden = [hidden, *fan(hidden, along_x)]
    values = fetch_sum(y_last[0], y_last[3], y_last[1], y_last[2], along_x)
    hidden, s_down, values = lax.optimization_barrier((hidden, s_down, values))
    hidden_last = activate(values, units, width)
    hidden_last = [hidden_last, *fan(hidden_last, along_x)]
    down_pieces = [w_mine, s_mine, d_behind, s_down, d_ahead, s_down, d_far, s_down]
    firsts = [wide, wide, 0, 0, 0, units, 0, wide]
    out = down(place, hidden, down_pieces, firsts, units)
    got = send(out[2], along_second(1)).astype(f32) + send(out[1], along_second(-1)).astype(f32)
    last = down(place, hidden_last, down_pieces, firsts, units)
    out = out[0].astype(f32) + (got + send(last[0], along_second(2)).astype(f32))
    own = out[0]
    out = out.astype(bf16)
    out = own + deliver(out[1], out[2], out[3], along_first)
    out = (mid_f + out).astype(bf16).reshape(SIDE, toks, part)
    pick = lambda d: lax.dynamic_index_in_dim(out, chips[order.index(d)], 0, False)
    far = send(pick(2), along_x(2))
    columns = jnp.stack([pick(0), send(pick(-1), along_x(-1)), far, send(pick(1), along_x(1))])
    columns = jnp.roll(columns, x, axis=0)
    return columns.transpose(1, 0, 2).reshape(toks, width)


def solution(mesh):
    return jax.shard_map(
        per_device,
        mesh=mesh,
        in_specs=(
            P(("seq", "exp"), None),
            P("seq", "exp"),
            P("seq", "exp"),
            P("seq", "exp"),
            P("seq", "exp"),
            P("exp", "seq"),
            P("exp"),
            P("exp", None),
            P(),
            P(("seq", "exp"), None),
            P(("seq", "exp"), None),
            P("exp", None, "seq"),
            P("exp", None, "seq"),
            P("exp", "seq", None),
        ),
        out_specs=P(("seq", "exp"), None),
        check_vma=False,
    )
```
